128 devices in a mesh: train: 32 (over z, y_lo, x), tp: 4 (over y_hi, core).
Axes of the slice: x: 4, y: 4 (y_hi: 2, y_lo: 2; y = y_hi * 2 + y_lo), z: 4, core: 2. Of those that a mesh axis runs over, the one named last changes fastest.
Arguments:
- offsets: int32 [3], replicated, may hold values from 1 to 127
- gate_flat: float32 [4, 44040192], P('tp', 'train'), may hold values from -0.0546875 to 0.0546875
- up_flat: float32 [4, 44040192], P('tp', 'train'), may hold values from -0.0546875 to 0.0546875
- down_flat: float32 [4, 44040192], P('tp', 'train'), may hold values from -0.046875 to 0.046875
- norm_gain: float32 [12288], replicated, may hold values from 0.1 to 1.9
- decode_state: bfloat16 [256, 12288], P(None, 'train'), may hold values from -33 to 33
Outputs:
- gate_codes: bfloat16 [14336, 12288], P('tp', 'train')
- gate_scales: float32 [14336, 96], P('tp', 'train')
- up_codes: bfloat16 [14336, 12288], P('tp', 'train')
- up_scales: float32 [14336, 96], P('tp', 'train')
- down_codes: bfloat16 [12288, 14336], P('train', 'tp')
- down_scales: float32 [12288, 112], P('train', 'tp')
- decoded: bfloat16 [256, 12288], P(None, 'train')
The draws below stay inside these ranges and needn't reach their ends.
All inputs are finite; a program needn't handle non-finite values. Where the reference program divides by a largest or mean magnitude, that divisor is 1e-20 or more.
Results may differ from the reference program's by a relative error of at most 0.025.
Values may be sent and summed in bfloat16 or wider, within the bound.
No kernel may reach another device: no remote copies, remote signals or barrier semaphores. Data moves between devices by JAX's collectives and lax.ppermute only.
A program may use at most 192 MiB of HBM per device.

```python
import jax
import jax.numpy as jnp
from jax import lax

D = 12288
FF = 14336
GROUP = 128
TOK = 256
STEPS = 3
FT = 3584
N_TP = 4


def draw_decode_state(key, part):
    key = jax.random.fold_in(key, 11)
    first, second, third = jax.random.split(key, 3)
    base = jnp.clip(jax.random.normal(first, (TOK, D), jnp.float32), -4.0, 4.0)
    row_log = jax.random.uniform(second, (TOK, 1), jnp.float32, -1.15, 1.15)
    ramp = jnp.linspace(-0.6, 0.6, D, dtype=jnp.float32)
    jitter = jax.random.uniform(third, (1, D), jnp.float32, -0.35, 0.35)
    return (base * jnp.exp(row_log + ramp[None, :] + jitter)).astype(jnp.bfloat16)


def steps_of(key, extent, cuts, least, high):
    factor_of, own = 1.0, jax.random.fold_in(key, 6)
    for dim, shards_of in cuts:
        draws = jnp.exp(jax.random.uniform(jax.random.fold_in(own, dim), (shards_of,), jnp.float32, least / len(cuts), high / len(cuts)))
        factor_of = factor_of * jnp.repeat(draws, extent[dim] // shards_of).reshape([-1 if axis == dim else 1 for axis in range(len(extent))])
    return factor_of


def gaussian(stream_key, dims, spread, reach, shards=(), held_as=jnp.bfloat16):
    result = jax.random.normal(stream_key, dims, jnp.float32) * spread
    if len(shards) > 0:
        result = steps_of(stream_key, dims, shards, -0.22, 0.18) * result
    return jnp.clip(result, min=-reach, max=reach).astype(held_as)


def setup_inputs(seed: int = 0) -> dict:
    keys = jax.random.split(jax.random.key(seed), 7)
    return {
        "offsets": jax.random.randint(keys[0], (3,), 1, GROUP).astype(jnp.int32),
        "gate_flat": gaussian(keys[1], (N_TP, FT * D), D ** -0.5, 0.0546875, ((0, 4), (1, 32)), jnp.float32),
        "up_flat": gaussian(keys[2], (N_TP, FT * D), D ** -0.5, 0.0546875, ((0, 4), (1, 32)), jnp.float32),
        "down_flat": gaussian(keys[3], (N_TP, D * FT), FF ** -0.5, 0.046875, ((0, 4), (1, 32)), jnp.float32),
        "norm_gain": jnp.clip(1.0 + 0.18 * jax.random.normal(keys[4], (D,), jnp.float32), 0.1, 1.9),
        "decode_state": draw_decode_state(jax.random.fold_in(keys[6], 71), 0),
    }


EPSILON_SCALE = 1e-06
EPSILON_NORM = 1e-05

def restore(buffer, offset):
    return jnp.roll(buffer, -offset, axis=1)

def quantize(matrix):
    count_rows, count_cols = matrix.shape
    grouped = matrix.reshape(count_rows, count_cols // GROUP, GROUP)
    scales = lax.optimization_barrier(jnp.max(jnp.abs(grouped), axis=2)) + EPSILON_SCALE
    codes = (grouped / scales[:, :, None]).astype(jnp.bfloat16)
    return (codes.reshape(count_rows, count_cols), scales)

def dequantize(codes, scales):
    count_rows, count_cols = codes.shape
    grouped = codes.astype(jnp.float32).reshape(count_rows, count_cols // GROUP, GROUP)
    return (grouped * scales[:, :, None]).astype(jnp.bfloat16).reshape(count_rows, count_cols)

def reference(offsets, gate_flat, up_flat, down_flat, norm_gain, decode_state):
    unit_count = FF // N_TP
    gate_weight = restore(gate_flat, offsets[0]).reshape(FF, D)
    up_weight = restore(up_flat, offsets[1]).reshape(FF, D)
    down_weight = restore(down_flat, offsets[2]).reshape(N_TP, D, unit_count)
    down_weight = jnp.transpose(down_weight, (1, 0, 2)).reshape(D, FF)
    gate_codes, gate_scales = quantize(gate_weight)
    up_codes, up_scales = quantize(up_weight)
    down_codes, down_scales = quantize(down_weight)
    gate_served = dequantize(gate_codes, gate_scales)
    up_served = dequantize(up_codes, up_scales)
    down_served = dequantize(down_codes, down_scales)
    state = decode_state
    for step in range(STEPS):
        wide = state.astype(jnp.float32)
        inverse = jax.lax.rsqrt(lax.optimization_barrier(jnp.mean(wide * wide, axis=1)) + EPSILON_NORM)
        scaled = (wide * norm_gain[None, :]).astype(jnp.bfloat16)
        gate = jnp.dot(scaled, gate_served.T, preferred_element_type=jnp.float32) * inverse[:, None]
        upper = jnp.dot(scaled, up_served.T, preferred_element_type=jnp.float32) * inverse[:, None]
        hidden = (jax.nn.silu(gate) * upper).astype(jnp.bfloat16)
        update = jnp.dot(hidden, down_served.T, preferred_element_type=jnp.float32)
        state = (wide + update).astype(jnp.bfloat16)
    return (gate_codes, gate_scales, up_codes, up_scales, down_codes, down_scales, state)
```

```python
import functools

import jax
import jax.numpy as jnp
from jax import lax
from jax.experimental import pallas as pl
from jax.experimental.pallas import tpu as pltpu
from jax.sharding import PartitionSpec as P

GROUP = 128
STEPS = 3
EPSILON_SCALE = 1e-06
EPSILON_NORM = 1e-05

N_Z = 4
N_Q = 8
N_TRAIN = N_Z * N_Q
ROWS = 112
PART = 384
PER = PART // GROUP
GROUPS_ROW = N_TRAIN * PER
BLOCK = 16
STRIP = 2 * ROWS + BLOCK
FT = ROWS * N_TRAIN
DOWN_GROUPS = FT // GROUP
DOWN_PER = DOWN_GROUPS // N_Z
DOWN_BLOCK = 64
DOWN_BLOCKS = PART // DOWN_BLOCK
TOK = 256
MSG = PART + BLOCK
VMEM_LIMIT = 28 * 1024 * 1024
HALF = TOK // 2
Z_HALF = N_Z // 2

bf16, f32 = jnp.bfloat16, jnp.float32


def params():
    return pltpu.CompilerParams(vmem_limit_bytes=VMEM_LIMIT)


def lanes_of(shape):
    return lax.broadcasted_iota(jnp.int32, shape, len(shape) - 1)


def following_rows(first, follow, turn):
    count = first.shape[0]
    up = pltpu.roll(first, count - 1, axis=0)
    row = lax.broadcasted_iota(jnp.int32, first.shape, 0)
    return pltpu.roll(jnp.where(row == count - 1, follow, up), turn, axis=1)


def realigned(x_ref, follow, turn, count, stride):
    lane = lanes_of((count, GROUP))
    own = lane < turn
    first = x_ref[pl.ds(0, count, stride=stride), :]
    current = pltpu.roll(first, turn, axis=1)
    for g in range(stride):
        if g + 1 < stride:
            after = pltpu.roll(x_ref[pl.ds(g + 1, count, stride=stride), :], turn, axis=1)
        else:
            after = following_rows(first, follow, turn)
        yield g, jnp.where(own, current, after)
        current = after


def scaled_group(group):
    scale = jnp.max(jnp.abs(group), axis=1, keepdims=True) + EPSILON_SCALE
    return scale, (group * (1.0 / scale)).astype(bf16)


def follow_of(step, last, next_ref, heads_ref, index):
    return jnp.where(step == last, heads_ref[index : index + 1, :], next_ref[0:1, :])


def pack_kernel(
    z_first, off_ref, gate_ref, gate_next, up_ref, up_next, heads_ref, out_ref, served_ref, kept_all, parts, rows
):
    step = pl.program_id(0)
    lane = lanes_of((ROWS, GROUP))
    last = (step == Z_HALF - 1) & (z_first > 0)
    kept_all[...] = jnp.zeros_like(kept_all)
    rows[...] = jnp.zeros_like(rows)
    for index, (x_ref, next_ref) in enumerate(((gate_ref, gate_next), (up_ref, up_next))):
        turn = GROUP - off_ref[index]
        own = lane < turn

        def turned(block):
            return pltpu.roll(block, turn, axis=1)

        after_row = next_ref[:, 0, :]
        wrapped = pltpu.roll(after_row, ROWS - 1, axis=0)
        row = lax.broadcasted_iota(jnp.int32, after_row.shape, 0)
        wrapped = jnp.where(row == ROWS - 1, heads_ref[index : index + 1, :], wrapped)
        follow = jnp.where(last, wrapped, after_row)
        kept = jnp.zeros((ROWS, GROUP), f32)
        current = turned(x_ref[:, 0, :])
        for g in range(N_Q * PER):
            after = turned(x_ref[:, g + 1, :] if g + 1 < N_Q * PER else follow)
            scale, codes = scaled_group(jnp.where(own, current, after))
            current = after
            q, k = g // PER, g % PER
            out_ref[q, 0, index * ROWS : (index + 1) * ROWS, k * GROUP : (k + 1) * GROUP] = codes
            served_ref[index * ROWS : (index + 1) * ROWS, g * GROUP : (g + 1) * GROUP] = (
                codes.astype(f32) * scale
            ).astype(bf16)
            kept = jnp.where(lane == q * 4 + k, scale, kept)
        kept_all[:ROWS, :] = kept
        rest = kept_all[...].T
        for part in range(3):
            piece = rest.astype(bf16).astype(f32)
            rest = rest - piece
            parts[...] = piece
            for k in range(PER):
                rows[k, pl.ds(index * 3 + part, N_Q, stride=BLOCK), :] = parts[pl.ds(k, N_Q, stride=4), :]
    for k in range(PER):
        out_ref[:, 0, 2 * ROWS :, k * GROUP : (k + 1) * GROUP] = (
            rows[k].reshape(N_Q, BLOCK, GROUP).astype(bf16)
        )


def pack(z_first, offsets, gate, up, heads):
    gate, up = (flat.reshape(ROWS, GROUPS_ROW, GROUP) for flat in (gate, up))
    part = N_Q * PER
    main = pl.BlockSpec((ROWS, part, GROUP), lambda s, off: (0, s + z_first, 0))
    after = pl.BlockSpec((ROWS, 8, GROUP), lambda s, off: (0, lax.rem((s + z_first + 1) * (part // 8), GROUPS_ROW // 8), 0))
    return pl.pallas_call(
        functools.partial(pack_kernel, z_first),
        out_shape=(
            jax.ShapeDtypeStruct((N_Q, Z_HALF, STRIP, PART), bf16),
            jax.ShapeDtypeStruct((2 * ROWS, Z_HALF * part * GROUP), bf16),
        ),
        grid_spec=pltpu.PrefetchScalarGridSpec(
            num_scalar_prefetch=1,
            grid=(Z_HALF,),
            in_specs=[main, after, main, after, pl.BlockSpec((8, GROUP), lambda s, off: (0, 0))],
            out_specs=(
                pl.BlockSpec((N_Q, 1, STRIP, PART), lambda s, off: (0, s, 0, 0)),
                pl.BlockSpec((2 * ROWS, part * GROUP), lambda s, off: (0, s)),
            ),
            scratch_shapes=[
                pltpu.VMEM((GROUP, GROUP), f32),
                pltpu.VMEM((GROUP, GROUP), f32),
                pltpu.VMEM((PER, N_Q * BLOCK, GROUP), f32),
            ],
        ),
        compiler_params=params(),
        name="pack_gate_up",
    )(offsets, gate, gate, up, up, heads)


def down_code_kernel(off_ref, place_ref, x_ref, next_ref, heads_ref, codes_ref, scales_ref, served_ref):
    step = pl.program_id(0)
    turn = GROUP - off_ref[2]
    follow = follow_of(step, DOWN_BLOCKS - 1, next_ref, heads_ref, 2)
    lane = lanes_of((DOWN_BLOCK, GROUP))
    kept = jnp.zeros((DOWN_BLOCK, GROUP), f32)
    for g, group in realigned(x_ref, follow, turn, DOWN_BLOCK, DOWN_GROUPS):
        scale, codes = scaled_group(group)
        codes_ref[:, g * GROUP : (g + 1) * GROUP] = codes
        z, k = g // DOWN_PER, g % DOWN_PER
        served_ref[lax.rem(z - place_ref[0] + N_Z, N_Z), :, k * GROUP : (k + 1) * GROUP] = (
            codes.astype(f32) * scale
        ).astype(bf16)
        kept = jnp.where(lane == g, scale, kept)
    scales_ref[...] = kept[:, :DOWN_GROUPS]


def code_down(offsets, place, down, heads):
    block_groups = DOWN_BLOCK * DOWN_GROUPS
    last = PART * DOWN_GROUPS // 8 - 1
    return pl.pallas_call(
        down_code_kernel,
        out_shape=(
            jax.ShapeDtypeStruct((PART, FT), bf16),
            jax.ShapeDtypeStruct((PART, DOWN_GROUPS), f32),
            jax.ShapeDtypeStruct((N_Z, PART, FT // N_Z), bf16),
        ),
        grid_spec=pltpu.PrefetchScalarGridSpec(
            num_scalar_prefetch=2,
            grid=(DOWN_BLOCKS,),
            in_specs=[
                pl.BlockSpec((block_groups, GROUP), lambda s, *_: (s, 0)),
                pl.BlockSpec((8, GROUP), lambda s, *_: (jnp.minimum((s + 1) * (block_groups // 8), last), 0)),
                pl.BlockSpec((8, GROUP), lambda s, *_: (0, 0)),
            ],
            out_specs=(
                pl.BlockSpec((DOWN_BLOCK, FT), lambda s, *_: (s, 0)),
                pl.BlockSpec((DOWN_BLOCK, DOWN_GROUPS), lambda s, *_: (s, 0)),
                pl.BlockSpec((N_Z, DOWN_BLOCK, FT // N_Z), lambda s, *_: (0, s, 0)),
            ),
        ),
        compiler_params=params(),
        name="code_down",
    )(offsets, place, down, down, heads)


def scale_columns(strip_of, count, gathered):
    gathered[...] = jnp.zeros_like(gathered)
    for n in range(count):
        tail = strip_of(n).astype(f32)
        for index in range(2):
            row = tail[3 * index : 3 * index + 1] + tail[3 * index + 1 : 3 * index + 2]
            row = row + tail[3 * index + 2 : 3 * index + 3]
            for k in range(PER):
                at = (n * 2 + index) * PER + k
                gathered[at : at + 1, :] = row[:, k * GROUP : (k + 1) * GROUP]
    return gathered[...].T


def serve_kernel(place_ref, in_ref, *refs):
    served_ref, gate_ref, up_ref, gathered = refs[-4:]
    columns = scale_columns(lambda n: in_ref[0, n, 2 * ROWS : STRIP, :], Z_HALF, gathered)
    for z in range(Z_HALF):
        gate_ref[z, 0] = in_ref[0, z, :ROWS]
        up_ref[z, 0] = in_ref[0, z, ROWS:]
        for index in range(2):
            for k in range(PER):
                at = (z * 2 + index) * PER + k
                codes = in_ref[0, z, index * ROWS : (index + 1) * ROWS, k * GROUP : (k + 1) * GROUP]
                served_ref[
                    index * ROWS : (index + 1) * ROWS, z * PART + k * GROUP : z * PART + (k + 1) * GROUP
                ] = (codes.astype(f32) * columns[:ROWS, at : at + 1]).astype(bf16)


def serve(half, place, strips, turned):
    return pl.pallas_call(
        serve_kernel,
        out_shape=(
            jax.ShapeDtypeStruct((N_Q * 2 * ROWS, Z_HALF * PART), bf16),
            jax.ShapeDtypeStruct((N_Z, N_Q, ROWS, PART), bf16),
            jax.ShapeDtypeStruct((N_Z, N_Q, STRIP - ROWS, PART), bf16),
        ),
        grid_spec=pltpu.PrefetchScalarGridSpec(
            num_scalar_prefetch=1,
            grid=(N_Q,),
            in_specs=[pl.BlockSpec((1, Z_HALF, STRIP, PART), lambda s, place: (s ^ place[1], 0, 0, 0))]
            + [pl.BlockSpec(memory_space=pl.ANY)] * len(turned),
            out_specs=(
                pl.BlockSpec((2 * ROWS, Z_HALF * PART), lambda s, place: (s, 0)),
                pl.BlockSpec((Z_HALF, 1, ROWS, PART), lambda s, place: (half, s ^ place[1], 0, 0)),
                pl.BlockSpec((Z_HALF, 1, STRIP - ROWS, PART), lambda s, place: (half, s ^ place[1], 0, 0)),
            ),
            scratch_shapes=[pltpu.VMEM((GROUP, GROUP), f32)],
        ),
        input_output_aliases={2 + n: 1 + n for n in range(len(turned))},
        compiler_params=params(),
        name="serve_gate_up",
    )(place, strips, *turned)


SPLIT = 4


def split_kernel(gate_in, up_in, gate_ref, gate_scales, up_ref, up_scales, gathered):
    columns = scale_columns(lambda n: up_in[n, ROWS:, :], SPLIT, gathered)
    for n in range(SPLIT):
        gate_ref[n * ROWS : (n + 1) * ROWS, :] = gate_in[n]
        up_ref[n * ROWS : (n + 1) * ROWS, :] = up_in[n, :ROWS]
        for index, scales in enumerate((gate_scales, up_scales)):
            at = (n * 2 + index) * PER
            scales[n * ROWS : (n + 1) * ROWS, :] = columns[:ROWS, at : at + PER]


def split(gate, up):
    codes = jax.ShapeDtypeStruct((FT, PART), bf16)
    scales = jax.ShapeDtypeStruct((FT, PER), f32)
    rows = SPLIT * ROWS
    return pl.pallas_call(
        split_kernel,
        out_shape=(codes, scales, codes, scales),
        grid=(N_TRAIN // SPLIT,),
        in_specs=[
            pl.BlockSpec((SPLIT, ROWS, PART), lambda s: (s, 0, 0)),
            pl.BlockSpec((SPLIT, STRIP - ROWS, PART), lambda s: (s, 0, 0)),
        ],
        out_specs=(
            pl.BlockSpec((rows, PART), lambda s: (s, 0)),
            pl.BlockSpec((rows, PER), lambda s: (s, 0)),
            pl.BlockSpec((rows, PART), lambda s: (s, 0)),
            pl.BlockSpec((rows, PER), lambda s: (s, 0)),
        ),
        scratch_shapes=[pltpu.VMEM((GROUP, GROUP), f32)],
        compiler_params=params(),
        name="split_gate_up",
    )(gate.reshape(N_TRAIN, ROWS, PART), up.reshape(N_TRAIN, STRIP - ROWS, PART))


def two_parts(row):
    high = row.astype(bf16).astype(f32)
    at = lax.broadcasted_iota(jnp.int32, (BLOCK, row.shape[1]), 0)
    return jnp.where(at == 0, high, jnp.where(at == 1, row - high, 0.0)).astype(bf16)


def message_of(state, gain):
    return (state * gain).astype(bf16), two_parts(jnp.sum(state * state, axis=0, keepdims=True))


SMEM_SPEC = pl.BlockSpec(memory_space=pltpu.SMEM)
VMEM_SPEC = pl.BlockSpec(memory_space=pltpu.VMEM)
ANY_SPEC = pl.BlockSpec(memory_space=pl.ANY)


def half_of(core):
    return pl.ds(pl.multiple_of(core * HALF, HALF), HALF)


def begin_kernel(place_ref, state_ref, gain_ref, heads_ref, state_out, out_ref):
    del heads_ref
    half = state_ref[half_of(place_ref[2]), :].astype(f32).T
    state_out[...] = half.astype(bf16)
    scaled, squares = message_of(half, gain_ref[...])
    for n in range(N_TRAIN):
        out_ref[n, :PART, :] = scaled
        out_ref[n, PART:, :] = squares


def begin(place, state, gain, heads):
    return pl.pallas_call(
        begin_kernel,
        out_shape=(
            jax.ShapeDtypeStruct((PART, HALF), bf16),
            jax.ShapeDtypeStruct((N_TRAIN, MSG, HALF), bf16),
        ),
        in_specs=[SMEM_SPEC, VMEM_SPEC, VMEM_SPEC, ANY_SPEC],
        compiler_params=params(),
        name="begin",
    )(place, state, gain, heads)


def release_kernel(*refs):
    del refs


def release(*arrays):
    return pl.pallas_call(
        release_kernel,
        out_shape=[jax.ShapeDtypeStruct(a.shape, a.dtype) for a in arrays],
        in_specs=[ANY_SPEC] * len(arrays),
        out_specs=[ANY_SPEC] * len(arrays),
        input_output_aliases={n: n for n in range(len(arrays))},
        compiler_params=params(),
        name="release",
    )(*arrays)


def activated(total, squares, width):
    inverse = lax.rsqrt(squares / width + EPSILON_NORM)
    gate = total[:ROWS] * inverse
    up = total[ROWS : 2 * ROWS] * inverse
    return (gate / (1.0 + jnp.exp(-gate)) * up).astype(bf16)


FIRST = 4


def first_kernel(width, place_ref, low_ref, high_ref, own_ref, other_ref, out_ref, total, squares):
    step = pl.program_id(0)
    in_low = step < N_TRAIN // FIRST // 2

    @pl.when(step == 0)
    def _():
        total[...] = jnp.zeros_like(total)
        squares[...] = jnp.zeros_like(squares)

    for side, x_ref in enumerate((own_ref, other_ref)):
        lanes = slice(side * HALF, (side + 1) * HALF)
        inputs = jnp.concatenate([x_ref[n, :PART, :] for n in range(FIRST)], axis=0)
        for near, weight_ref in ((in_low, low_ref), (~in_low, high_ref)):

            @pl.when(near)
            def _():
                total[:, lanes] += jnp.dot(weight_ref[...], inputs, preferred_element_type=f32)

        for n in range(FIRST):
            tail = x_ref[n, PART:, :].astype(f32)
            squares[0:1, lanes] += tail[0:1] + tail[1:2]

    @pl.when(step == N_TRAIN // FIRST - 1)
    def _():
        hidden = activated(total[...], squares[0:1, :], width)
        core = place_ref[2]
        for side in range(2):
            at = pl.multiple_of((core ^ side) * HALF, HALF)
            out_ref[:, pl.ds(at, HALF)] = hidden[:, side * HALF : (side + 1) * HALF]


def first_hidden(place, low, high, own, other, width):
    inputs = pl.BlockSpec((FIRST, MSG, HALF), lambda s, place: (s, 0, 0))
    steps = N_TRAIN // FIRST
    return pl.pallas_call(
        functools.partial(first_kernel, float(width)),
        out_shape=jax.ShapeDtypeStruct((ROWS, TOK), bf16),
        grid_spec=pltpu.PrefetchScalarGridSpec(
            num_scalar_prefetch=1,
            grid=(steps,),
            in_specs=[
                pl.BlockSpec((2 * ROWS, FIRST * PART), lambda s, place: (0, jnp.minimum(s, steps // 2 - 1))),
                pl.BlockSpec((2 * ROWS, FIRST * PART), lambda s, place: (0, jnp.maximum(s - steps // 2, 0))),
                inputs,
                inputs,
            ],
            out_specs=pl.BlockSpec((ROWS, TOK), lambda s, place: (0, 0)),
            scratch_shapes=[pltpu.VMEM((2 * ROWS, TOK), f32), pltpu.VMEM((8, TOK), f32)],
        ),
        compiler_params=params(),
        name="first_hidden",
    )(place, low, high, own, other)


def terms_kernel(place_ref, low_ref, high_ref, *refs):
    own, other, outs, inputs = refs[:N_Z], refs[N_Z : 2 * N_Z], refs[-N_Q - 2 : -2], refs[-1]
    core = place_ref[2]
    squares = []
    for side, messages in enumerate((own, other)):
        lanes = half_of(core ^ side)
        total = jnp.zeros((1, HALF), f32)
        for d, message in enumerate(messages):
            at = pl.multiple_of(lax.rem(place_ref[0] - d + N_Z, N_Z) * PART, PART)
            inputs[pl.ds(at, PART), lanes] = message[:PART, :]
            tail = message[PART:, :].astype(f32)
            total += tail[0:1] + tail[1:2]
        squares.append(total)
    middle = Z_HALF * PART
    for d, out in enumerate(outs):
        rows = slice(d * 2 * ROWS, (d + 1) * 2 * ROWS)
        total = jnp.dot(low_ref[rows, :], inputs[:middle, :], preferred_element_type=f32)
        total += jnp.dot(high_ref[rows, :], inputs[middle:, :], preferred_element_type=f32)
        out[: 2 * ROWS, :] = total.astype(bf16)
        for side in range(2):
            out[2 * ROWS :, half_of(core ^ side)] = two_parts(squares[side])


def gate_up_terms(place, low, high, own, other, held):
    return pl.pallas_call(
        terms_kernel,
        out_shape=[jax.ShapeDtypeStruct((STRIP, TOK), bf16)] * N_Q
        + [jax.ShapeDtypeStruct(held.shape, held.dtype)],
        in_specs=[SMEM_SPEC] + [VMEM_SPEC] * (2 + 2 * N_Z) + [ANY_SPEC],
        out_specs=[VMEM_SPEC] * N_Q + [ANY_SPEC],
        scratch_shapes=[pltpu.VMEM((N_Z * PART, TOK), bf16)],
        input_output_aliases={3 + 2 * N_Z: N_Q},
        compiler_params=params(),
        name="gate_up_terms",
    )(place, low, high, *own, *other, held)


def hidden_kernel(width, *refs):
    total = refs[0][...].astype(f32)
    for term in refs[1:-1]:
        total += term[...].astype(f32)
    squares = total[2 * ROWS : 2 * ROWS + 1] + total[2 * ROWS + 1 : 2 * ROWS + 2]
    refs[-1][...] = activated(total, squares, width)


def hidden_of(terms, width):
    return pl.pallas_call(
        functools.partial(hidden_kernel, float(width)),
        out_shape=jax.ShapeDtypeStruct((ROWS, TOK), bf16),
        compiler_params=params(),
        name="hidden",
    )(*terms)


def update_kernel(place_ref, *refs):
    hidden, weights = refs[:N_Q], refs[N_Q : N_Q + N_Z]
    keep_ref, send_ref, joined, result = refs[-4:]
    for d, block in enumerate(hidden):
        at = pl.multiple_of((place_ref[1] ^ d) * ROWS, BLOCK)
        joined[pl.ds(at, ROWS), :] = block[...]
    core = place_ref[2]
    for d, weight in enumerate(weights):
        result[d] = jnp.dot(weight[...], joined[...], preferred_element_type=f32).astype(bf16)
        keep_ref[d] = result[d, :, half_of(core)]
        send_ref[d] = result[d, :, half_of(core ^ 1)]


def update_terms(place, hidden, weights):
    return pl.pallas_call(
        update_kernel,
        out_shape=[jax.ShapeDtypeStruct((N_Z, PART, HALF), bf16)] * 2,
        in_specs=[SMEM_SPEC] + [VMEM_SPEC] * (N_Q + N_Z),
        scratch_shapes=[pltpu.VMEM((FT // N_Z, TOK), bf16), pltpu.VMEM((N_Z, PART, TOK), bf16)],
        compiler_params=params(),
        name="update_terms",
    )(place, *hidden, *weights)


def pair_kernel(own_ref, other_ref, *refs):
    for d, out in enumerate(refs[-N_Z:]):
        out[...] = (own_ref[d].astype(f32) + other_ref[d].astype(f32)).astype(bf16)


def pair_sums(own, other, after):
    return pl.pallas_call(
        pair_kernel,
        out_shape=[jax.ShapeDtypeStruct((PART, HALF), bf16)] * N_Z,
        in_specs=[VMEM_SPEC, VMEM_SPEC] + [ANY_SPEC] * len(after),
        compiler_params=params(),
        name="pair_sums",
    )(own, other, *after)


def sum_kernel(*refs):
    total = refs[0][...].astype(f32)
    for term in refs[1:-1]:
        total += term[...].astype(f32)
    refs[-1][...] = total.astype(bf16)


def sum_of(terms):
    return pl.pallas_call(
        sum_kernel,
        out_shape=jax.ShapeDtypeStruct((PART, HALF), bf16),
        compiler_params=params(),
        name="sum_over_z",
    )(*terms)


def advance_kernel(state_ref, own_ref, other_ref, gain_ref, next_ref, msg_ref):
    update = own_ref[...].astype(f32) + other_ref[...].astype(f32)
    state = (state_ref[...].astype(f32) + update).astype(bf16)
    next_ref[...] = state
    scaled, squares = message_of(state.astype(f32), gain_ref[...])
    msg_ref[:PART, :] = scaled
    msg_ref[PART:, :] = squares


def advance(state, own, other, gain):
    return pl.pallas_call(
        advance_kernel,
        out_shape=(jax.ShapeDtypeStruct((PART, HALF), bf16), jax.ShapeDtypeStruct((MSG, HALF), bf16)),
        compiler_params=params(),
        name="advance",
    )(state, own, other, gain)


def finish_kernel(place_ref, *refs):
    out_ref = refs[-1]
    for side in range(2):
        state, own, other = refs[3 * side : 3 * side + 3]
        update = own[...].astype(f32) + other[...].astype(f32)
        out_ref[half_of(place_ref[2] ^ side), :] = (state[...].astype(f32) + update).T.astype(bf16)


def finish(place, *sides):
    return pl.pallas_call(
        finish_kernel,
        out_shape=jax.ShapeDtypeStruct((TOK, PART), bf16),
        in_specs=[SMEM_SPEC] + [VMEM_SPEC] * 6,
        compiler_params=params(),
        name="finish",
    )(place, *sides)


def along_z(block, d):
    route = [(z * N_Q + q, (z + d) % N_Z * N_Q + q) for z in range(N_Z) for q in range(N_Q)]
    return lax.ppermute(block, "train", route)


def across_q(block, d):
    return lax.ppermute(block, "train", [(i, i ^ d) for i in range(N_TRAIN)])


def across_tp(block, d):
    return lax.ppermute(block, "tp", [(t, t ^ d) for t in range(4)])


def body(offsets, gate_flat, up_flat, down_flat, norm_gain, decode_state):
    width = norm_gain.shape[0]
    index = lax.axis_index("train")
    place = jnp.stack([index // N_Q, index % N_Q, lax.axis_index("tp") % 2]).astype(jnp.int32)
    q_groups = [[z * N_Q + q for q in range(N_Q)] for z in range(N_Z)]
    z_groups = [[z * N_Q + q for z in range(N_Z)] for q in range(N_Q)]

    heads = jnp.concatenate(
        [gate_flat[:, :GROUP], up_flat[:, :GROUP], down_flat[:, :GROUP], jnp.zeros((5, GROUP), f32)]
    )
    heads = lax.ppermute(heads, "train", [((i + 1) % N_TRAIN, i) for i in range(N_TRAIN)])
    gain = lax.dynamic_slice_in_dim(norm_gain, index * PART, PART, 0).reshape(PART, 1)
    state, first = begin(place, decode_state, gain, heads)
    first = lax.all_to_all(first, "train", 0, 0, tiled=True)

    gate, up, down = (flat.reshape(-1, GROUP) for flat in (gate_flat, up_flat, down_flat))
    low_strips, low_first = pack(0, offsets, gate, up, heads)
    high_strips, high_first = pack(Z_HALF, offsets, gate, up, heads)
    down_codes, down_scales, down_served = code_down(offsets, place, down, heads)
    first, low_strips, down_served = release(first, low_strips, down_served)
    low_strips = lax.all_to_all(low_strips, "train", 0, 0, axis_index_groups=q_groups, tiled=True)
    down_weights = [down_served[0]] + [along_z(down_served[d], d) for d in range(1, N_Z)]
    hidden = first_hidden(place, low_first, high_first, first, across_tp(first, 1), width)
    hidden, low_strips = release(hidden, low_strips)

    owned = []
    for step in range(STEPS):
        if step > 0:
            own = [message] + [along_z(message, d) for d in range(1, N_Z)]
            other = [across_tp(m, 1) for m in own]
            *terms, held = gate_up_terms(place, low_served, high_served, own, other, turned[step - 1])
            owned.append(lax.all_to_all(held, "train", 0, 0, axis_index_groups=z_groups, tiled=True))
            hidden = hidden_of([terms[0]] + [across_q(terms[d], d) for d in range(1, N_Q)], width)
        blocks = [hidden] + [across_q(hidden, d) for d in range(1, N_Q)]
        keep, send = update_terms(place, blocks, down_weights)
        if step == 0:
            keep, high_strips = release(keep, high_strips)
            high_strips = lax.all_to_all(high_strips, "train", 0, 0, axis_index_groups=q_groups, tiled=True)
            low_served, *turned = serve(0, place, low_strips, ())
            high_served, *turned = serve(1, place, high_strips, turned)
        sums = pair_sums(keep, across_tp(send, 1), owned[-1:])
        own = sum_of([sums[0]] + [along_z(sums[d], -d) for d in range(1, N_Z)])
        if step < STEPS - 1:
            state, message = advance(state, own, across_tp(own, 2), gain)
        else:
            decoded = finish(
                place, state, own, across_tp(own, 2), across_tp(state, 1), across_tp(own, 1), across_tp(own, 3)
            )
    gate_codes, gate_scales, up_codes, up_scales = split(*owned)
    return (gate_codes, gate_scales, up_codes, up_scales, down_codes, down_scales, decoded)


def solution(mesh):
    in_specs = (P(), P("tp", "train"), P("tp", "train"), P("tp", "train"), P(), P(None, "train"))
    out_specs = (
        P("tp", "train"),
        P("tp", "train"),
        P("tp", "train"),
        P("tp", "train"),
        P("train", "tp"),
        P("train", "tp"),
        P(None, "train"),
    )
    return jax.shard_map(body, mesh=mesh, in_specs=in_specs, out_specs=out_specs, check_vma=False)
```

```python
import functools

import jax
import jax.numpy as jnp
from jax import lax
from jax.experimental import pallas as pl
from jax.experimental.pallas import tpu as pltpu
from jax.sharding import PartitionSpec as P

GROUP = 128
STEPS = 3
EPSILON_SCALE = 1e-06
EPSILON_NORM = 1e-05

N_Z = 4
N_Q = 8
N_TRAIN = N_Z * N_Q
ROWS = 112
PART = 384
PER = PART // GROUP
GROUPS_ROW = N_TRAIN * PER
BLOCK = 16
STRIP = 2 * ROWS + BLOCK
FT = ROWS * N_TRAIN
DOWN_GROUPS = FT // GROUP
DOWN_PER = DOWN_GROUPS // N_Z
DOWN_BLOCK = 128
DOWN_BLOCKS = PART // DOWN_BLOCK
TOK = 256
MSG = PART + BLOCK
MIB = 1024 * 1024
HALF = TOK // 2
Z_HALF = N_Z // 2

bf16, f32 = jnp.bfloat16, jnp.float32


def params(mib=16):
    return pltpu.CompilerParams(vmem_limit_bytes=mib * MIB)


SMEM_SPEC = pl.BlockSpec(memory_space=pltpu.SMEM)
VMEM_SPEC = pl.BlockSpec(memory_space=pltpu.VMEM)
ANY_SPEC = pl.BlockSpec(memory_space=pl.ANY)


def in_hbm(array):
    return pltpu.with_memory_space_constraint(array, pltpu.HBM)


def in_vmem(array):
    return pltpu.with_memory_space_constraint(array, pltpu.VMEM)


def lanes_of(shape):
    return lax.broadcasted_iota(jnp.int32, shape, len(shape) - 1)


def following_rows(first, follow, turn):
    count = first.shape[0]
    up = pltpu.roll(first, count - 1, axis=0)
    row = lax.broadcasted_iota(jnp.int32, first.shape, 0)
    return pltpu.roll(jnp.where(row == count - 1, follow, up), turn, axis=1)


def scaled_group(group):
    scale = jnp.max(jnp.abs(group), axis=1, keepdims=True) + EPSILON_SCALE
    return scale, (group * (1.0 / scale)).astype(bf16)


def follow_of(step, last, next_ref, heads_ref, index):
    return jnp.where(step == last, heads_ref[index : index + 1, :], next_ref[0:1, :])


def pack_kernel(
    z_first, off_ref, gate_ref, gate_next, up_ref, up_next, heads_ref, out_ref, served_ref, kept_all, parts, rows
):
    step = pl.program_id(0)
    lane = lanes_of((ROWS, GROUP))
    last = (step == Z_HALF - 1) & (z_first > 0)
    kept_all[...] = jnp.zeros_like(kept_all)
    rows[...] = jnp.zeros_like(rows)
    for index, (x_ref, next_ref) in enumerate(((gate_ref, gate_next), (up_ref, up_next))):
        turn = GROUP - off_ref[index]
        own = lane < turn

        def turned(block):
            return pltpu.roll(block, turn, axis=1)

        after_row = next_ref[:, 0, :]
        wrapped = pltpu.roll(after_row, ROWS - 1, axis=0)
        row = lax.broadcasted_iota(jnp.int32, after_row.shape, 0)
        wrapped = jnp.where(row == ROWS - 1, heads_ref[index : index + 1, :], wrapped)
        follow = jnp.where(last, wrapped, after_row)
        kept = jnp.zeros((ROWS, GROUP), f32)
        current = turned(x_ref[:, 0, :])
        for g in range(N_Q * PER):
            after = turned(x_ref[:, g + 1, :] if g + 1 < N_Q * PER else follow)
            scale, codes = scaled_group(jnp.where(own, current, after))
            current = after
            q, k = g // PER, g % PER
            out_ref[q, 0, index * ROWS : (index + 1) * ROWS, k * GROUP : (k + 1) * GROUP] = codes
            served_ref[index * ROWS : (index + 1) * ROWS, g * GROUP : (g + 1) * GROUP] = (
                codes.astype(f32) * scale
            ).astype(bf16)
            kept = jnp.where(lane == q * 4 + k, scale, kept)
        kept_all[:ROWS, :] = kept
        rest = kept_all[...].T
        for part in range(3):
            piece = rest.astype(bf16).astype(f32)
            rest = rest - piece
            parts[...] = piece
            for k in range(PER):
                rows[k, pl.ds(index * 3 + part, N_Q, stride=BLOCK), :] = parts[pl.ds(k, N_Q, stride=4), :]
    for k in range(PER):
        out_ref[:, 0, 2 * ROWS :, k * GROUP : (k + 1) * GROUP] = (
            rows[k].reshape(N_Q, BLOCK, GROUP).astype(bf16)
        )


def pack(z_first, offsets, gate, up, heads):
    gate, up = (in_hbm(flat.reshape(ROWS, GROUPS_ROW, GROUP)) for flat in (gate, up))
    part = N_Q * PER
    main = pl.BlockSpec((ROWS, part, GROUP), lambda s, off: (0, s + z_first, 0))
    after = pl.BlockSpec((ROWS, 8, GROUP), lambda s, off: (0, lax.rem((s + z_first + 1) * (part // 8), GROUPS_ROW // 8), 0))
    return pl.pallas_call(
        functools.partial(pack_kernel, z_first),
        out_shape=(
            pltpu.HBM((N_Q, Z_HALF, STRIP, PART), bf16),
            pltpu.HBM((2 * ROWS, Z_HALF * part * GROUP), bf16),
        ),
        grid_spec=pltpu.PrefetchScalarGridSpec(
            num_scalar_prefetch=1,
            grid=(Z_HALF,),
            in_specs=[main, after, main, after, pl.BlockSpec((8, GROUP), lambda s, off: (0, 0))],
            out_specs=(
                pl.BlockSpec((N_Q, 1, STRIP, PART), lambda s, off: (0, s, 0, 0)),
                pl.BlockSpec((2 * ROWS, part * GROUP), lambda s, off: (0, s)),
            ),
            scratch_shapes=[
                pltpu.VMEM((GROUP, GROUP), f32),
                pltpu.VMEM((GROUP, GROUP), f32),
                pltpu.VMEM((PER, N_Q * BLOCK, GROUP), f32),
            ],
        ),
        compiler_params=params(24),
        name="pack_gate_up",
    )(offsets, gate, gate, up, up, heads)


def down_code_kernel(off_ref, place_ref, x_ref, next_ref, heads_ref, *refs):
    codes_ref, scales_ref, *served = refs[-2 - N_Z :]
    step = pl.program_id(0)
    turn = GROUP - off_ref[2]
    lane = lanes_of((DOWN_BLOCK, GROUP))
    own = lane < turn
    kept = jnp.zeros((DOWN_BLOCK, GROUP), f32)

    def column(g):
        return x_ref[pl.ds(g, DOWN_BLOCK, stride=DOWN_GROUPS), :]

    follow = follow_of(step, DOWN_BLOCKS - 1, next_ref, heads_ref, 2)
    wrapped = following_rows(column(0), follow, turn)
    for d, out in enumerate(served):
        z = lax.rem(place_ref[0] + d, N_Z)
        base = z * DOWN_PER
        current = pltpu.roll(column(base), turn, axis=1)
        for k in range(DOWN_PER):
            g = base + k
            if k + 1 < DOWN_PER:
                after = pltpu.roll(column(g + 1), turn, axis=1)
            else:
                after = pltpu.roll(column(jnp.minimum(g + 1, DOWN_GROUPS - 1)), turn, axis=1)
                after = jnp.where(z == N_Z - 1, wrapped, after)
            scale, codes = scaled_group(jnp.where(own, current, after))
            current = after
            codes_ref[:, pl.ds(pl.multiple_of(g * GROUP, GROUP), GROUP)] = codes
            out[:, k * GROUP : (k + 1) * GROUP] = (codes.astype(f32) * scale).astype(bf16)
            kept = jnp.where(lane == g, scale, kept)
    scales_ref[...] = kept.T[:DOWN_GROUPS, :]


def code_down(offsets, place, down, heads, after):
    block_groups = DOWN_BLOCK * DOWN_GROUPS
    last = PART * DOWN_GROUPS // 8 - 1
    return pl.pallas_call(
        down_code_kernel,
        out_shape=[
            jax.ShapeDtypeStruct((PART, FT), bf16),
            jax.ShapeDtypeStruct((DOWN_GROUPS, PART), f32),
        ]
        + [pltpu.HBM((PART, FT // N_Z), bf16)] * N_Z,
        grid_spec=pltpu.PrefetchScalarGridSpec(
            num_scalar_prefetch=2,
            grid=(DOWN_BLOCKS,),
            in_specs=[
                pl.BlockSpec((block_groups, GROUP), lambda s, *_: (s, 0)),
                pl.BlockSpec((8, GROUP), lambda s, *_: (jnp.minimum((s + 1) * (block_groups // 8), last), 0)),
                pl.BlockSpec((8, GROUP), lambda s, *_: (0, 0)),
            ]
            + [pl.BlockSpec(memory_space=pl.ANY)] * len(after),
            out_specs=[
                pl.BlockSpec((DOWN_BLOCK, FT), lambda s, *_: (s, 0)),
                pl.BlockSpec((DOWN_GROUPS, DOWN_BLOCK), lambda s, *_: (0, s)),
            ]
            + [pl.BlockSpec((DOWN_BLOCK, FT // N_Z), lambda s, *_: (s, 0))] * N_Z,
        ),
        compiler_params=params(),
        name="code_down",
    )(offsets, place, down, down, heads, *map(in_hbm, after))


def scale_columns(strip_of, count, gathered):
    gathered[...] = jnp.zeros_like(gathered)
    for n in range(count):
        tail = strip_of(n).astype(f32)
        for index in range(2):
            row = tail[3 * index : 3 * index + 1] + tail[3 * index + 1 : 3 * index + 2]
            row = row + tail[3 * index + 2 : 3 * index + 3]
            for k in range(PER):
                at = (n * 2 + index) * PER + k
                gathered[at : at + 1, :] = row[:, k * GROUP : (k + 1) * GROUP]
    return gathered[...].T


def serve_kernel(place_ref, in_ref, *refs):
    served_ref, gate_ref, up_ref, gathered = refs[-4:]
    columns = scale_columns(lambda n: in_ref[0, n, 2 * ROWS : STRIP, :], Z_HALF, gathered)
    for z in range(Z_HALF):
        gate_ref[z, 0] = in_ref[0, z, :ROWS]
        up_ref[z, 0] = in_ref[0, z, ROWS:]
        for index in range(2):
            for k in range(PER):
                at = (z * 2 + index) * PER + k
                codes = in_ref[0, z, index * ROWS : (index + 1) * ROWS, k * GROUP : (k + 1) * GROUP]
                served_ref[
                    index * ROWS : (index + 1) * ROWS, z * PART + k * GROUP : z * PART + (k + 1) * GROUP
                ] = (codes.astype(f32) * columns[:ROWS, at : at + 1]).astype(bf16)


def serve(half, place, strips, turned):
    return pl.pallas_call(
        serve_kernel,
        out_shape=(
            pltpu.VMEM((N_Q * 2 * ROWS, Z_HALF * PART), bf16),
            pltpu.HBM((N_Z, N_Q, ROWS, PART), bf16),
            pltpu.HBM((N_Z, N_Q, STRIP - ROWS, PART), bf16),
        ),
        grid_spec=pltpu.PrefetchScalarGridSpec(
            num_scalar_prefetch=1,
            grid=(N_Q,),
            in_specs=[pl.BlockSpec((1, Z_HALF, STRIP, PART), lambda s, place: (s ^ place[1], 0, 0, 0))]
            + [pl.BlockSpec(memory_space=pl.ANY)] * len(turned),
            out_specs=(
                pl.BlockSpec((2 * ROWS, Z_HALF * PART), lambda s, place: (s, 0)),
                pl.BlockSpec((Z_HALF, 1, ROWS, PART), lambda s, place: (half, s ^ place[1], 0, 0)),
                pl.BlockSpec((Z_HALF, 1, STRIP - ROWS, PART), lambda s, place: (half, s ^ place[1], 0, 0)),
            ),
            scratch_shapes=[pltpu.VMEM((GROUP, GROUP), f32)],
        ),
        input_output_aliases={2 + n: 1 + n for n in range(len(turned))},
        compiler_params=params(),
        name="serve_gate_up",
    )(place, in_hbm(strips), *turned)


SPLIT = 8


def scale_row(tail, index):
    parts = tail[3 * index : 3 * index + 3].astype(f32)
    return parts[0:1] + parts[1:2] + parts[2:3]


def split_kernel(gate_in, up_in, gate_ref, gate_scales, up_ref, up_scales, rows):
    lane = lanes_of((8, GROUP))
    blocks = SPLIT * ROWS // GROUP
    for index, scales in enumerate((gate_scales, up_scales)):
        sums = [jnp.zeros((8, GROUP), f32) for _ in range(blocks)]
        for n in range(SPLIT):
            row = scale_row(up_in[n, ROWS:, :], index)
            rows[...] = jnp.zeros_like(rows)
            for k in range(PER):
                rows[k : k + 1, :] = row[:, k * GROUP : (k + 1) * GROUP]
            block, offset = n * ROWS // GROUP, n * ROWS % GROUP
            moved = jnp.where(lane < ROWS, rows[...], 0.0)
            moved = pltpu.roll(moved, offset, axis=1) if offset else moved
            sums[block] = sums[block] + jnp.where(lane >= offset, moved, 0.0)
            if offset + ROWS > GROUP:
                sums[block + 1] = sums[block + 1] + jnp.where(lane < offset, moved, 0.0)
        for block in range(blocks):
            scales[:, block * GROUP : (block + 1) * GROUP] = sums[block][:PER, :]
    for n in range(SPLIT):
        gate_ref[n * ROWS : (n + 1) * ROWS, :] = gate_in[n]
        up_ref[n * ROWS : (n + 1) * ROWS, :] = up_in[n, :ROWS]


def split(gate, up):
    codes = pltpu.HBM((FT, PART), bf16)
    scales = pltpu.HBM((PER, FT), f32)
    rows = SPLIT * ROWS
    return pl.pallas_call(
        split_kernel,
        out_shape=(codes, scales, codes, scales),
        grid=(N_TRAIN // SPLIT,),
        in_specs=[
            pl.BlockSpec((SPLIT, ROWS, PART), lambda s: (s, 0, 0)),
            pl.BlockSpec((SPLIT, STRIP - ROWS, PART), lambda s: (s, 0, 0)),
        ],
        out_specs=(
            pl.BlockSpec((rows, PART), lambda s: (s, 0)),
            pl.BlockSpec((PER, rows), lambda s: (0, s)),
            pl.BlockSpec((rows, PART), lambda s: (s, 0)),
            pl.BlockSpec((PER, rows), lambda s: (0, s)),
        ),
        scratch_shapes=[pltpu.VMEM((8, GROUP), f32)],
        compiler_params=params(),
        name="split_gate_up",
    )(in_hbm(gate.reshape(N_TRAIN, ROWS, PART)), in_hbm(up.reshape(N_TRAIN, STRIP - ROWS, PART)))


def two_parts(row):
    high = row.astype(bf16).astype(f32)
    at = lax.broadcasted_iota(jnp.int32, (BLOCK, row.shape[1]), 0)
    return jnp.where(at == 0, high, jnp.where(at == 1, row - high, 0.0)).astype(bf16)


def message_of(state, gain, refs):
    scaled, squares = (state * gain).astype(bf16), two_parts(jnp.sum(state * state, axis=0, keepdims=True))
    for ref in refs:
        ref[:PART, :] = scaled
        ref[PART:, :] = squares


def both(shape):
    return pltpu.HBM(shape, bf16), pltpu.VMEM(shape, bf16)


def half_of(core):
    return pl.ds(pl.multiple_of(core * HALF, HALF), HALF)


def begin_kernel(place_ref, state_ref, gain_ref, heads_ref, state_out, out_ref):
    del heads_ref
    half = state_ref[half_of(place_ref[2]), :].astype(f32).T
    state_out[...] = half.astype(bf16)
    message_of(half, gain_ref[...], [out_ref.at[n] for n in range(N_TRAIN)])


def begin(place, state, gain, heads):
    return pl.pallas_call(
        begin_kernel,
        out_shape=(pltpu.VMEM((PART, HALF), bf16), pltpu.HBM((N_TRAIN, MSG, HALF), bf16)),
        in_specs=[SMEM_SPEC, VMEM_SPEC, VMEM_SPEC, ANY_SPEC],
        compiler_params=params(),
        name="begin",
    )(place, state, gain, in_hbm(heads))


def release_kernel(*refs):
    del refs


def release(arrays, after):
    return pl.pallas_call(
        release_kernel,
        out_shape=[pltpu.HBM(a.shape, a.dtype) for a in arrays],
        in_specs=[ANY_SPEC] * (len(arrays) + len(after)),
        out_specs=[ANY_SPEC] * len(arrays),
        input_output_aliases={n: n for n in range(len(arrays))},
        compiler_params=params(),
        name="release",
    )(*arrays, *map(in_hbm, after))


def activated(total, squares, width):
    inverse = lax.rsqrt(squares / width + EPSILON_NORM)
    gate = total[:ROWS] * inverse
    up = total[ROWS : 2 * ROWS] * inverse
    return (gate / (1.0 + jnp.exp(-gate)) * up).astype(bf16)


FIRST = 4


def first_kernel(width, place_ref, low_ref, high_ref, own_ref, other_ref, *refs):
    outs, (total, squares) = refs[:2], refs[2:]
    step = pl.program_id(0)
    in_low = step < N_TRAIN // FIRST // 2

    @pl.when(step == 0)
    def _():
        total[...] = jnp.zeros_like(total)
        squares[...] = jnp.zeros_like(squares)

    for side, x_ref in enumerate((own_ref, other_ref)):
        lanes = slice(side * HALF, (side + 1) * HALF)
        inputs = jnp.concatenate([x_ref[n, :PART, :] for n in range(FIRST)], axis=0)
        for near, weight_ref in ((in_low, low_ref), (~in_low, high_ref)):

            @pl.when(near)
            def _():
                total[:, lanes] += jnp.dot(weight_ref[...], inputs, preferred_element_type=f32)

        for n in range(FIRST):
            tail = x_ref[n, PART:, :].astype(f32)
            squares[0:1, lanes] += tail[0:1] + tail[1:2]

    @pl.when(step == N_TRAIN // FIRST - 1)
    def _():
        hidden = activated(total[...], squares[0:1, :], width)
        core = place_ref[2]
        for side in range(2):
            at = pl.multiple_of((core ^ side) * HALF, HALF)
            for out in outs:
                out[:, pl.ds(at, HALF)] = hidden[:, side * HALF : (side + 1) * HALF]


def first_hidden(place, low, high, own, other, width):
    inputs = pl.BlockSpec((FIRST, MSG, HALF), lambda s, place: (s, 0, 0))
    steps = N_TRAIN // FIRST
    return pl.pallas_call(
        functools.partial(first_kernel, float(width)),
        out_shape=both((ROWS, TOK)),
        grid_spec=pltpu.PrefetchScalarGridSpec(
            num_scalar_prefetch=1,
            grid=(steps,),
            in_specs=[
                pl.BlockSpec((2 * ROWS, FIRST * PART), lambda s, place: (0, jnp.minimum(s, steps // 2 - 1))),
                pl.BlockSpec((2 * ROWS, FIRST * PART), lambda s, place: (0, jnp.maximum(s - steps // 2, 0))),
                inputs,
                inputs,
            ],
            out_specs=[pl.BlockSpec((ROWS, TOK), lambda s, place: (0, 0))] * 2,
            scratch_shapes=[pltpu.VMEM((2 * ROWS, TOK), f32), pltpu.VMEM((8, TOK), f32)],
        ),
        compiler_params=params(),
        name="first_hidden",
    )(place, *map(in_hbm, (low, high, own, other)))


def terms_kernel(place_ref, low_ref, high_ref, *refs):
    own, other, outs, inputs = refs[:N_Z], refs[N_Z : 2 * N_Z], refs[-N_Q - 2 : -2], refs[-1]
    core = place_ref[2]
    squares = []
    for side, messages in enumerate((own, other)):
        lanes = half_of(core ^ side)
        total = jnp.zeros((1, HALF), f32)
        for d, message in enumerate(messages):
            at = pl.multiple_of(lax.rem(place_ref[0] - d + N_Z, N_Z) * PART, PART)
            inputs[pl.ds(at, PART), lanes] = message[:PART, :]
            tail = message[PART:, :].astype(f32)
            total += tail[0:1] + tail[1:2]
        squares.append(total)
    middle = Z_HALF * PART
    for d, out in enumerate(outs):
        rows = slice(d * 2 * ROWS, (d + 1) * 2 * ROWS)
        total = jnp.dot(low_ref[rows, :], inputs[:middle, :], preferred_element_type=f32)
        total += jnp.dot(high_ref[rows, :], inputs[middle:, :], preferred_element_type=f32)
        out[: 2 * ROWS, :] = total.astype(bf16)
        for side in range(2):
            out[2 * ROWS :, half_of(core ^ side)] = two_parts(squares[side])


def gate_up_terms(place, low, high, own, other, held):
    return pl.pallas_call(
        terms_kernel,
        out_shape=[pltpu.VMEM((STRIP, TOK), bf16)]
        + [pltpu.HBM((STRIP, TOK), bf16)] * (N_Q - 1)
        + [pltpu.HBM(held.shape, held.dtype)],
        in_specs=[SMEM_SPEC] + [VMEM_SPEC] * (2 + 2 * N_Z) + [ANY_SPEC],
        out_specs=[VMEM_SPEC] * N_Q + [ANY_SPEC],
        scratch_shapes=[pltpu.VMEM((N_Z * PART, TOK), bf16)],
        input_output_aliases={3 + 2 * N_Z: N_Q},
        compiler_params=params(),
        name="gate_up_terms",
    )(place, in_vmem(low), in_vmem(high), *own, *other, held)


def hidden_kernel(width, *refs):
    total = refs[0][...].astype(f32)
    for term in refs[1:N_Q]:
        total += term[...].astype(f32)
    squares = total[2 * ROWS : 2 * ROWS + 1] + total[2 * ROWS + 1 : 2 * ROWS + 2]
    hidden = activated(total, squares, width)
    for out in refs[N_Q:]:
        out[...] = hidden


def hidden_of(terms, width):
    return pl.pallas_call(
        functools.partial(hidden_kernel, float(width)),
        out_shape=both((ROWS, TOK)),
        compiler_params=params(),
        name="hidden",
    )(*terms)


def update_kernel(place_ref, *refs):
    hidden, weights = refs[:N_Q], refs[N_Q : N_Q + N_Z]
    send_ref, keep_ref, joined, result = refs[-4:]
    for d, block in enumerate(hidden):
        at = pl.multiple_of((place_ref[1] ^ d) * ROWS, BLOCK)
        joined[pl.ds(at, ROWS), :] = block[...]
    core = place_ref[2]
    for d, weight in enumerate(weights):
        result[d] = jnp.dot(weight[...], joined[...], preferred_element_type=f32).astype(bf16)
        send_ref[d] = result[d, :, half_of(core ^ 1)]
        keep_ref[d] = result[d, :, half_of(core)]


def update_terms(place, hidden, weights, after):
    return pl.pallas_call(
        update_kernel,
        out_shape=both((N_Z, PART, HALF)),
        in_specs=[SMEM_SPEC] + [VMEM_SPEC] * (N_Q + N_Z) + [ANY_SPEC] * len(after),
        scratch_shapes=[pltpu.VMEM((FT // N_Z, TOK), bf16), pltpu.VMEM((N_Z, PART, TOK), bf16)],
        compiler_params=params(),
        name="update_terms",
    )(place, *hidden, *weights, *map(in_hbm, after))


def pair_kernel(own_ref, other_ref, *refs):
    for d, out in enumerate(refs[-N_Z:]):
        out[...] = (own_ref[d].astype(f32) + other_ref[d].astype(f32)).astype(bf16)


def pair_sums(own, other, after):
    return pl.pallas_call(
        pair_kernel,
        out_shape=[pltpu.VMEM((PART, HALF), bf16)] + [pltpu.HBM((PART, HALF), bf16)] * (N_Z - 1),
        in_specs=[VMEM_SPEC, VMEM_SPEC] + [ANY_SPEC] * len(after),
        compiler_params=params(),
        name="pair_sums",
    )(own, other, *map(in_hbm, after))


def sum_kernel(*refs):
    total = refs[0][...].astype(f32)
    for term in refs[1:N_Z]:
        total += term[...].astype(f32)
    for out in refs[N_Z:]:
        out[...] = total.astype(bf16)


def sum_of(terms):
    return pl.pallas_call(
        sum_kernel,
        out_shape=both((PART, HALF)),
        compiler_params=params(),
        name="sum_over_z",
    )(*terms)


def advance_kernel(state_ref, own_ref, other_ref, gain_ref, *refs):
    next_send, next_ref, *messages = refs[-4:]
    update = own_ref[...].astype(f32) + other_ref[...].astype(f32)
    state = (state_ref[...].astype(f32) + update).astype(bf16)
    next_send[...] = state
    next_ref[...] = state
    message_of(state.astype(f32), gain_ref[...], messages)


def advance(state, own, other, gain, after):
    return pl.pallas_call(
        advance_kernel,
        out_shape=(*both((PART, HALF)), *both((MSG, HALF))),
        in_specs=[VMEM_SPEC] * 4 + [ANY_SPEC] * len(after),
        compiler_params=params(),
        name="advance",
    )(state, own, other, gain, *map(in_hbm, after))


def finish_kernel(place_ref, *refs):
    out_ref = refs[-1]
    for side in range(2):
        state, own, other = refs[3 * side : 3 * side + 3]
        update = own[...].astype(f32) + other[...].astype(f32)
        out_ref[half_of(place_ref[2] ^ side), :] = (state[...].astype(f32) + update).T.astype(bf16)


def finish(place, *sides):
    return pl.pallas_call(
        finish_kernel,
        out_shape=jax.ShapeDtypeStruct((TOK, PART), bf16),
        in_specs=[SMEM_SPEC] + [VMEM_SPEC] * 6,
        compiler_params=params(),
        name="finish",
    )(place, *sides)


def along_z(block, d):
    route = [(z * N_Q + q, (z + d) % N_Z * N_Q + q) for z in range(N_Z) for q in range(N_Q)]
    return lax.ppermute(block, "train", route)


def across_q(block, d):
    return lax.ppermute(block, "train", [(i, i ^ d) for i in range(N_TRAIN)])


def across_tp(block, d):
    return lax.ppermute(block, "tp", [(t, t ^ d) for t in range(4)])


def body(offsets, gate_flat, up_flat, down_flat, norm_gain, decode_state):
    width = norm_gain.shape[0]
    index = lax.axis_index("train")
    place = jnp.stack([index // N_Q, index % N_Q, lax.axis_index("tp") % 2]).astype(jnp.int32)
    q_groups = [[z * N_Q + q for q in range(N_Q)] for z in range(N_Z)]
    z_groups = [[z * N_Q + q for z in range(N_Z)] for q in range(N_Q)]

    heads = jnp.concatenate(
        [gate_flat[:, :GROUP], up_flat[:, :GROUP], down_flat[:, :GROUP], jnp.zeros((5, GROUP), f32)]
    )
    heads = lax.ppermute(heads, "train", [((i + 1) % N_TRAIN, i) for i in range(N_TRAIN)])
    gain = lax.dynamic_slice_in_dim(norm_gain, index * PART, PART, 0).reshape(PART, 1)
    state, first = begin(place, decode_state, gain, heads)
    first = lax.all_to_all(first, "train", 0, 0, tiled=True)

    gate, up, down = (flat.reshape(-1, GROUP) for flat in (gate_flat, up_flat, down_flat))
    low_strips, low_first = pack(0, offsets, gate, up, heads)
    high_strips, high_first = pack(Z_HALF, offsets, gate, up, heads)
    down_codes, down_scales, *down_served = code_down(offsets, place, down, heads, ())
    first, low_strips, *sent = release((first, low_strips, *down_served[1:]), (high_strips, high_first))
    other_first = across_tp(first, 1)
    low_strips = lax.all_to_all(low_strips, "train", 0, 0, axis_index_groups=q_groups, tiled=True)
    down_weights = [down_served[0]] + [along_z(sent[d - 1], d) for d in range(1, N_Z)]
    hidden, hidden_own = first_hidden(place, low_first, high_first, first, other_first, width)

    owned = []
    for step in range(STEPS):
        if step > 0:
            received = [along_z(message, d) for d in range(1, N_Z)]
            others = [across_tp(m, 1) for m in (message, *received)]
            *terms, held = gate_up_terms(
                place, low_served, high_served, (message_own, *received), others, turned[step - 1]
            )
            owned.append(lax.all_to_all(held, "train", 0, 0, axis_index_groups=z_groups, tiled=True))
            hidden, hidden_own = hidden_of([terms[0]] + [across_q(terms[d], d) for d in range(1, N_Q)], width)
        blocks = [hidden_own] + [across_q(hidden, d) for d in range(1, N_Q)]
        send, keep = update_terms(place, blocks, down_weights, ())
        after = ()
        if step == 0:
            (high_strips,) = release((high_strips,), (send,))
            high_strips = lax.all_to_all(high_strips, "train", 0, 0, axis_index_groups=q_groups, tiled=True)
            low_served, *turned = serve(0, place, low_strips, ())
            after = turned[:1]
            high_served, *turned = serve(1, place, high_strips, turned)
        sums = pair_sums(keep, across_tp(send, 1), owned[-1:])
        total, total_own = sum_of([sums[0]] + [along_z(sums[d], -d) for d in range(1, N_Z)])
        other = across_tp(total, 2)
        if step < STEPS - 1:
            state_send, state, message, message_own = advance(state, total_own, other, gain, after)
        else:
            sides = (across_tp(state_send, 1), across_tp(total, 1), across_tp(total, 3))
            decoded = finish(place, state, total_own, other, *sides)
    gate_codes, gate_scales, up_codes, up_scales = split(*owned)
    return (gate_codes, gate_scales.T, up_codes, up_scales.T, down_codes, down_scales.T, decoded)


def solution(mesh):
    in_specs = (P(), P("tp", "train"), P("tp", "train"), P("tp", "train"), P(), P(None, "train"))
    out_specs = (
        P("tp", "train"),
        P("tp", "train"),
        P("tp", "train"),
        P("tp", "train"),
        P("train", "tp"),
        P("train", "tp"),
        P(None, "train"),
    )
    return jax.shard_map(body, mesh=mesh, in_specs=in_specs, out_specs=out_specs, check_vma=False)
```

```python
import functools

import jax
import jax.numpy as jnp
from jax import lax
from jax.experimental import pallas as pl
from jax.experimental.pallas import tpu as pltpu
from jax.sharding import PartitionSpec as P

GROUP = 128
STEPS = 3
EPSILON_SCALE = 1e-06
EPSILON_NORM = 1e-05

N_Z = 4
N_Q = 8
N_TRAIN = N_Z * N_Q
ROWS = 112
PART = 384
PER = PART // GROUP
GROUPS_ROW = N_TRAIN * PER
BLOCK = 16
STRIP = 2 * ROWS + BLOCK
FT = ROWS * N_TRAIN
DOWN_GROUPS = FT // GROUP
DOWN_PER = DOWN_GROUPS // N_Z
DOWN_BLOCK = 128
DOWN_BLOCKS = PART // DOWN_BLOCK
TOK = 256
MSG = PART + BLOCK
MIB = 1024 * 1024
HALF = TOK // 2
Z_HALF = N_Z // 2

bf16, f32 = jnp.bfloat16, jnp.float32


def params(mib=16):
    return pltpu.CompilerParams(vmem_limit_bytes=mib * MIB)


SMEM_SPEC = pl.BlockSpec(memory_space=pltpu.SMEM)
VMEM_SPEC = pl.BlockSpec(memory_space=pltpu.VMEM)
ANY_SPEC = pl.BlockSpec(memory_space=pl.ANY)


def in_hbm(array):
    return pltpu.with_memory_space_constraint(array, pltpu.HBM)


def in_vmem(array):
    return pltpu.with_memory_space_constraint(array, pltpu.VMEM)


def lanes_of(shape):
    return lax.broadcasted_iota(jnp.int32, shape, len(shape) - 1)


def following_rows(first, follow, turn):
    count = first.shape[0]
    up = pltpu.roll(first, count - 1, axis=0)
    row = lax.broadcasted_iota(jnp.int32, first.shape, 0)
    return pltpu.roll(jnp.where(row == count - 1, follow, up), turn, axis=1)


def scaled_group(group):
    scale = jnp.max(jnp.abs(group), axis=1, keepdims=True) + EPSILON_SCALE
    return scale, (group * (1.0 / scale)).astype(bf16)


def follow_of(step, last, next_ref, heads_ref, index):
    return jnp.where(step == last, heads_ref[index : index + 1, :], next_ref[0:1, :])


def pack_kernel(
    z_first, off_ref, gate_ref, gate_next, up_ref, up_next, heads_ref, out_ref, served_ref, kept_all, parts, rows
):
    step = pl.program_id(0)
    lane = lanes_of((ROWS, GROUP))
    last = (step == Z_HALF - 1) & (z_first > 0)
    kept_all[...] = jnp.zeros_like(kept_all)
    rows[...] = jnp.zeros_like(rows)
    for index, (x_ref, next_ref) in enumerate(((gate_ref, gate_next), (up_ref, up_next))):
        turn = GROUP - off_ref[index]
        own = lane < turn

        def turned(block):
            return pltpu.roll(block, turn, axis=1)

        after_row = next_ref[:, 0, :]
        wrapped = pltpu.roll(after_row, ROWS - 1, axis=0)
        row = lax.broadcasted_iota(jnp.int32, after_row.shape, 0)
        wrapped = jnp.where(row == ROWS - 1, heads_ref[index : index + 1, :], wrapped)
        follow = jnp.where(last, wrapped, after_row)
        kept = jnp.zeros((ROWS, GROUP), f32)
        current = turned(x_ref[:, 0, :])
        for g in range(N_Q * PER):
            after = turned(x_ref[:, g + 1, :] if g + 1 < N_Q * PER else follow)
            scale, codes = scaled_group(jnp.where(own, current, after))
            current = after
            q, k = g // PER, g % PER
            out_ref[q, 0, index * ROWS : (index + 1) * ROWS, k * GROUP : (k + 1) * GROUP] = codes
            served_ref[index * ROWS : (index + 1) * ROWS, g * GROUP : (g + 1) * GROUP] = (
                codes.astype(f32) * scale
            ).astype(bf16)
            kept = jnp.where(lane == q * 4 + k, scale, kept)
        kept_all[:ROWS, :] = kept
        rest = kept_all[...].T
        for part in range(3):
            piece = rest.astype(bf16).astype(f32)
            rest = rest - piece
            parts[...] = piece
            for k in range(PER):
                rows[k, pl.ds(index * 3 + part, N_Q, stride=BLOCK), :] = parts[pl.ds(k, N_Q, stride=4), :]
    for k in range(PER):
        out_ref[:, 0, 2 * ROWS :, k * GROUP : (k + 1) * GROUP] = (
            rows[k].reshape(N_Q, BLOCK, GROUP).astype(bf16)
        )


def pack(z_first, offsets, gate, up, heads):
    gate, up = (in_hbm(flat.reshape(ROWS, GROUPS_ROW, GROUP)) for flat in (gate, up))
    part = N_Q * PER
    main = pl.BlockSpec((ROWS, part, GROUP), lambda s, off: (0, s + z_first, 0))
    after = pl.BlockSpec((ROWS, 8, GROUP), lambda s, off: (0, lax.rem((s + z_first + 1) * (part // 8), GROUPS_ROW // 8), 0))
    return pl.pallas_call(
        functools.partial(pack_kernel, z_first),
        out_shape=(
            pltpu.HBM((N_Q, Z_HALF, STRIP, PART), bf16),
            pltpu.HBM((2 * ROWS, Z_HALF * part * GROUP), bf16),
        ),
        grid_spec=pltpu.PrefetchScalarGridSpec(
            num_scalar_prefetch=1,
            grid=(Z_HALF,),
            in_specs=[main, after, main, after, pl.BlockSpec((8, GROUP), lambda s, off: (0, 0))],
            out_specs=(
                pl.BlockSpec((N_Q, 1, STRIP, PART), lambda s, off: (0, s, 0, 0)),
                pl.BlockSpec((2 * ROWS, part * GROUP), lambda s, off: (0, s)),
            ),
            scratch_shapes=[
                pltpu.VMEM((GROUP, GROUP), f32),
                pltpu.VMEM((GROUP, GROUP), f32),
                pltpu.VMEM((PER, N_Q * BLOCK, GROUP), f32),
            ],
        ),
        compiler_params=params(24),
        name="pack_gate_up",
    )(offsets, gate, gate, up, up, heads)


def down_code_kernel(off_ref, place_ref, x_ref, next_ref, heads_ref, *refs):
    codes_ref, scales_ref, *served = refs[-2 - N_Z :]
    step = pl.program_id(0)
    turn = GROUP - off_ref[2]
    lane = lanes_of((DOWN_BLOCK, GROUP))
    own = lane < turn
    kept = jnp.zeros((DOWN_BLOCK, GROUP), f32)

    def column(g):
        return x_ref[pl.ds(g, DOWN_BLOCK, stride=DOWN_GROUPS), :]

    follow = follow_of(step, DOWN_BLOCKS - 1, next_ref, heads_ref, 2)
    wrapped = following_rows(column(0), follow, turn)
    for d, out in enumerate(served):
        z = lax.rem(place_ref[0] + d, N_Z)
        base = z * DOWN_PER
        current = pltpu.roll(column(base), turn, axis=1)
        for k in range(DOWN_PER):
            g = base + k
            if k + 1 < DOWN_PER:
                after = pltpu.roll(column(g + 1), turn, axis=1)
            else:
                after = pltpu.roll(column(jnp.minimum(g + 1, DOWN_GROUPS - 1)), turn, axis=1)
                after = jnp.where(z == N_Z - 1, wrapped, after)
            scale, codes = scaled_group(jnp.where(own, current, after))
            current = after
            codes_ref[:, pl.ds(pl.multiple_of(g * GROUP, GROUP), GROUP)] = codes
            out[:, k * GROUP : (k + 1) * GROUP] = (codes.astype(f32) * scale).astype(bf16)
            kept = jnp.where(lane == g, scale, kept)
    scales_ref[...] = kept.T[:DOWN_GROUPS, :]


def code_down(offsets, place, down, heads, after):
    block_groups = DOWN_BLOCK * DOWN_GROUPS
    last = PART * DOWN_GROUPS // 8 - 1
    return pl.pallas_call(
        down_code_kernel,
        out_shape=[
            jax.ShapeDtypeStruct((PART, FT), bf16),
            jax.ShapeDtypeStruct((DOWN_GROUPS, PART), f32),
        ]
        + [pltpu.HBM((PART, FT // N_Z), bf16)] * N_Z,
        grid_spec=pltpu.PrefetchScalarGridSpec(
            num_scalar_prefetch=2,
            grid=(DOWN_BLOCKS,),
            in_specs=[
                pl.BlockSpec((block_groups, GROUP), lambda s, *_: (s, 0)),
                pl.BlockSpec((8, GROUP), lambda s, *_: (jnp.minimum((s + 1) * (block_groups // 8), last), 0)),
                pl.BlockSpec((8, GROUP), lambda s, *_: (0, 0)),
            ]
            + [pl.BlockSpec(memory_space=pl.ANY)] * len(after),
            out_specs=[
                pl.BlockSpec((DOWN_BLOCK, FT), lambda s, *_: (s, 0)),
                pl.BlockSpec((DOWN_GROUPS, DOWN_BLOCK), lambda s, *_: (0, s)),
            ]
            + [pl.BlockSpec((DOWN_BLOCK, FT // N_Z), lambda s, *_: (s, 0))] * N_Z,
        ),
        compiler_params=params(),
        name="code_down",
    )(offsets, place, down, down, heads, *map(in_hbm, after))


def scale_columns(strip_of, count, gathered):
    gathered[...] = jnp.zeros_like(gathered)
    for n in range(count):
        tail = strip_of(n).astype(f32)
        for index in range(2):
            row = tail[3 * index : 3 * index + 1] + tail[3 * index + 1 : 3 * index + 2]
            row = row + tail[3 * index + 2 : 3 * index + 3]
            for k in range(PER):
                at = (n * 2 + index) * PER + k
                gathered[at : at + 1, :] = row[:, k * GROUP : (k + 1) * GROUP]
    return gathered[...].T


def serve_kernel(place_ref, in_ref, *refs):
    served_ref, gate_ref, up_ref, gathered = refs[-4:]
    columns = scale_columns(lambda n: in_ref[0, n, 2 * ROWS : STRIP, :], Z_HALF, gathered)
    for z in range(Z_HALF):
        gate_ref[z, 0] = in_ref[0, z, :ROWS]
        up_ref[z, 0] = in_ref[0, z, ROWS:]
        for index in range(2):
            for k in range(PER):
                at = (z * 2 + index) * PER + k
                codes = in_ref[0, z, index * ROWS : (index + 1) * ROWS, k * GROUP : (k + 1) * GROUP]
                served_ref[
                    index * ROWS : (index + 1) * ROWS, z * PART + k * GROUP : z * PART + (k + 1) * GROUP
                ] = (codes.astype(f32) * columns[:ROWS, at : at + 1]).astype(bf16)


def serve(half, place, strips, turned):
    return pl.pallas_call(
        serve_kernel,
        out_shape=(
            pltpu.VMEM((N_Q * 2 * ROWS, Z_HALF * PART), bf16),
            pltpu.HBM((N_Z, N_Q, ROWS, PART), bf16),
            pltpu.HBM((N_Z, N_Q, STRIP - ROWS, PART), bf16),
        ),
        grid_spec=pltpu.PrefetchScalarGridSpec(
            num_scalar_prefetch=1,
            grid=(N_Q,),
            in_specs=[pl.BlockSpec((1, Z_HALF, STRIP, PART), lambda s, place: (s ^ place[1], 0, 0, 0))]
            + [pl.BlockSpec(memory_space=pl.ANY)] * len(turned),
            out_specs=(
                pl.BlockSpec((2 * ROWS, Z_HALF * PART), lambda s, place: (s, 0)),
                pl.BlockSpec((Z_HALF, 1, ROWS, PART), lambda s, place: (half, s ^ place[1], 0, 0)),
                pl.BlockSpec((Z_HALF, 1, STRIP - ROWS, PART), lambda s, place: (half, s ^ place[1], 0, 0)),
            ),
            scratch_shapes=[pltpu.VMEM((GROUP, GROUP), f32)],
        ),
        input_output_aliases={2 + n: 1 + n for n in range(len(turned))},
        compiler_params=params(),
        name="serve_gate_up",
    )(place, in_hbm(strips), *turned)


SPLIT = 8


def scale_row(tail, index):
    parts = tail[3 * index : 3 * index + 3].astype(f32)
    return parts[0:1] + parts[1:2] + parts[2:3]


def split_kernel(gate_in, up_in, gate_ref, gate_scales, up_ref, up_scales, rows):
    lane = lanes_of((8, GROUP))
    blocks = SPLIT * ROWS // GROUP
    for index, scales in enumerate((gate_scales, up_scales)):
        sums = [jnp.zeros((8, GROUP), f32) for _ in range(blocks)]
        for n in range(SPLIT):
            row = scale_row(up_in[n, ROWS:, :], index)
            rows[...] = jnp.zeros_like(rows)
            for k in range(PER):
                rows[k : k + 1, :] = row[:, k * GROUP : (k + 1) * GROUP]
            block, offset = n * ROWS // GROUP, n * ROWS % GROUP
            moved = jnp.where(lane < ROWS, rows[...], 0.0)
            moved = pltpu.roll(moved, offset, axis=1) if offset else moved
            sums[block] = sums[block] + jnp.where(lane >= offset, moved, 0.0)
            if offset + ROWS > GROUP:
                sums[block + 1] = sums[block + 1] + jnp.where(lane < offset, moved, 0.0)
        for block in range(blocks):
            scales[:, block * GROUP : (block + 1) * GROUP] = sums[block][:PER, :]
    for n in range(SPLIT):
        gate_ref[n * ROWS : (n + 1) * ROWS, :] = gate_in[n]
        up_ref[n * ROWS : (n + 1) * ROWS, :] = up_in[n, :ROWS]


def split(gate, up):
    codes = pltpu.HBM((FT, PART), bf16)
    scales = pltpu.HBM((PER, FT), f32)
    rows = SPLIT * ROWS
    return pl.pallas_call(
        split_kernel,
        out_shape=(codes, scales, codes, scales),
        grid=(N_TRAIN // SPLIT,),
        in_specs=[
            pl.BlockSpec((SPLIT, ROWS, PART), lambda s: (s, 0, 0)),
            pl.BlockSpec((SPLIT, STRIP - ROWS, PART), lambda s: (s, 0, 0)),
        ],
        out_specs=(
            pl.BlockSpec((rows, PART), lambda s: (s, 0)),
            pl.BlockSpec((PER, rows), lambda s: (0, s)),
            pl.BlockSpec((rows, PART), lambda s: (s, 0)),
            pl.BlockSpec((PER, rows), lambda s: (0, s)),
        ),
        scratch_shapes=[pltpu.VMEM((8, GROUP), f32)],
        compiler_params=params(),
        name="split_gate_up",
    )(in_hbm(gate.reshape(N_TRAIN, ROWS, PART)), in_hbm(up.reshape(N_TRAIN, STRIP - ROWS, PART)))


def two_parts(row):
    high = row.astype(bf16).astype(f32)
    at = lax.broadcasted_iota(jnp.int32, (BLOCK, row.shape[1]), 0)
    return jnp.where(at == 0, high, jnp.where(at == 1, row - high, 0.0)).astype(bf16)


def message_of(state, gain, refs):
    scaled, squares = (state * gain).astype(bf16), two_parts(jnp.sum(state * state, axis=0, keepdims=True))
    for ref in refs:
        ref[:PART, :] = scaled
        ref[PART:, :] = squares


def both(shape):
    return pltpu.HBM(shape, bf16), pltpu.VMEM(shape, bf16)


def half_of(core):
    return pl.ds(pl.multiple_of(core * HALF, HALF), HALF)


def begin_kernel(place_ref, state_ref, gain_ref, state_out, out_ref):
    half = state_ref[half_of(place_ref[2]), :].astype(f32).T
    state_out[...] = half.astype(bf16)
    message_of(half, gain_ref[...], [out_ref.at[n] for n in range(N_TRAIN)])


def begin(place, state, gain):
    return pl.pallas_call(
        begin_kernel,
        out_shape=(pltpu.HBM((PART, HALF), bf16), pltpu.HBM((N_TRAIN, MSG, HALF), bf16)),
        in_specs=[SMEM_SPEC, VMEM_SPEC, VMEM_SPEC],
        compiler_params=params(),
        name="begin",
    )(place, state, gain)


def release_kernel(*refs):
    del refs


def release(arrays, after):
    return pl.pallas_call(
        release_kernel,
        out_shape=[pltpu.HBM(a.shape, a.dtype) for a in arrays],
        in_specs=[ANY_SPEC] * (len(arrays) + len(after)),
        out_specs=[ANY_SPEC] * len(arrays),
        input_output_aliases={n: n for n in range(len(arrays))},
        compiler_params=params(),
        name="release",
    )(*arrays, *map(in_hbm, after))


def activated(total, squares, width):
    inverse = lax.rsqrt(squares / width + EPSILON_NORM)
    gate = total[:ROWS] * inverse
    up = total[ROWS : 2 * ROWS] * inverse
    return (gate / (1.0 + jnp.exp(-gate)) * up).astype(bf16)


FIRST = 4


def first_kernel(width, place_ref, low_ref, high_ref, own_ref, other_ref, *refs):
    outs, (total, squares) = refs[:2], refs[2:]
    step = pl.program_id(0)
    in_low = step < N_TRAIN // FIRST // 2

    @pl.when(step == 0)
    def _():
        total[...] = jnp.zeros_like(total)
        squares[...] = jnp.zeros_like(squares)

    for side, x_ref in enumerate((own_ref, other_ref)):
        lanes = slice(side * HALF, (side + 1) * HALF)
        inputs = jnp.concatenate([x_ref[n, :PART, :] for n in range(FIRST)], axis=0)
        for near, weight_ref in ((in_low, low_ref), (~in_low, high_ref)):

            @pl.when(near)
            def _():
                total[:, lanes] += jnp.dot(weight_ref[...], inputs, preferred_element_type=f32)

        for n in range(FIRST):
            tail = x_ref[n, PART:, :].astype(f32)
            squares[0:1, lanes] += tail[0:1] + tail[1:2]

    @pl.when(step == N_TRAIN // FIRST - 1)
    def _():
        hidden = activated(total[...], squares[0:1, :], width)
        core = place_ref[2]
        for side in range(2):
            at = pl.multiple_of((core ^ side) * HALF, HALF)
            for out in outs:
                out[:, pl.ds(at, HALF)] = hidden[:, side * HALF : (side + 1) * HALF]


def first_hidden(place, low, high, own, other, width):
    inputs = pl.BlockSpec((FIRST, MSG, HALF), lambda s, place: (s, 0, 0))
    steps = N_TRAIN // FIRST
    return pl.pallas_call(
        functools.partial(first_kernel, float(width)),
        out_shape=both((ROWS, TOK)),
        grid_spec=pltpu.PrefetchScalarGridSpec(
            num_scalar_prefetch=1,
            grid=(steps,),
            in_specs=[
                pl.BlockSpec((2 * ROWS, FIRST * PART), lambda s, place: (0, jnp.minimum(s, steps // 2 - 1))),
                pl.BlockSpec((2 * ROWS, FIRST * PART), lambda s, place: (0, jnp.maximum(s - steps // 2, 0))),
                inputs,
                inputs,
            ],
            out_specs=[pl.BlockSpec((ROWS, TOK), lambda s, place: (0, 0))] * 2,
            scratch_shapes=[pltpu.VMEM((2 * ROWS, TOK), f32), pltpu.VMEM((8, TOK), f32)],
        ),
        compiler_params=params(),
        name="first_hidden",
    )(place, *map(in_hbm, (low, high, own, other)))


def terms_kernel(place_ref, low_ref, high_ref, *refs):
    own, other, outs, inputs = refs[:N_Z], refs[N_Z : 2 * N_Z], refs[-N_Q - 2 : -2], refs[-1]
    core = place_ref[2]
    squares = []
    for side, messages in enumerate((own, other)):
        lanes = half_of(core ^ side)
        total = jnp.zeros((1, HALF), f32)
        for d, message in enumerate(messages):
            at = pl.multiple_of(lax.rem(place_ref[0] - d + N_Z, N_Z) * PART, PART)
            inputs[pl.ds(at, PART), lanes] = message[:PART, :]
            tail = message[PART:, :].astype(f32)
            total += tail[0:1] + tail[1:2]
        squares.append(total)
    middle = Z_HALF * PART
    for d, out in enumerate(outs):
        rows = slice(d * 2 * ROWS, (d + 1) * 2 * ROWS)
        total = jnp.dot(low_ref[rows, :], inputs[:middle, :], preferred_element_type=f32)
        total += jnp.dot(high_ref[rows, :], inputs[middle:, :], preferred_element_type=f32)
        out[: 2 * ROWS, :] = total.astype(bf16)
        for side in range(2):
            out[2 * ROWS :, half_of(core ^ side)] = two_parts(squares[side])


def gate_up_terms(place, low, high, own, other, held):
    return pl.pallas_call(
        terms_kernel,
        out_shape=[pltpu.VMEM((STRIP, TOK), bf16)]
        + [pltpu.HBM((STRIP, TOK), bf16)] * (N_Q - 1)
        + [pltpu.HBM(held.shape, held.dtype)],
        in_specs=[SMEM_SPEC] + [VMEM_SPEC] * (2 + 2 * N_Z) + [ANY_SPEC],
        out_specs=[VMEM_SPEC] * N_Q + [ANY_SPEC],
        scratch_shapes=[pltpu.VMEM((N_Z * PART, TOK), bf16)],
        input_output_aliases={3 + 2 * N_Z: N_Q},
        compiler_params=params(),
        name="gate_up_terms",
    )(place, in_vmem(low), in_vmem(high), *own, *other, held)


def hidden_kernel(width, *refs):
    total = refs[0][...].astype(f32)
    for term in refs[1:N_Q]:
        total += term[...].astype(f32)
    squares = total[2 * ROWS : 2 * ROWS + 1] + total[2 * ROWS + 1 : 2 * ROWS + 2]
    hidden = activated(total, squares, width)
    for out in refs[N_Q:]:
        out[...] = hidden


def hidden_of(terms, width):
    return pl.pallas_call(
        functools.partial(hidden_kernel, float(width)),
        out_shape=both((ROWS, TOK)),
        compiler_params=params(),
        name="hidden",
    )(*terms)


def update_kernel(place_ref, *refs):
    hidden, weights = refs[:N_Q], refs[N_Q : N_Q + N_Z]
    send_ref, keep_ref, joined, result = refs[-4:]
    for d, block in enumerate(hidden):
        at = pl.multiple_of((place_ref[1] ^ d) * ROWS, BLOCK)
        joined[pl.ds(at, ROWS), :] = block[...]
    core = place_ref[2]
    for d, weight in enumerate(weights):
        result[d] = jnp.dot(weight[...], joined[...], preferred_element_type=f32).astype(bf16)
        send_ref[d] = result[d, :, half_of(core ^ 1)]
        keep_ref[d] = result[d, :, half_of(core)]


def update_terms(place, hidden, weights, kept):
    return pl.pallas_call(
        update_kernel,
        out_shape=(pltpu.HBM((N_Z, PART, HALF), bf16), kept((N_Z, PART, HALF), bf16)),
        in_specs=[SMEM_SPEC] + [VMEM_SPEC] * (N_Q + N_Z),
        scratch_shapes=[pltpu.VMEM((FT // N_Z, TOK), bf16), pltpu.VMEM((N_Z, PART, TOK), bf16)],
        compiler_params=params(),
        name="update_terms",
    )(place, *hidden, *weights)


def pair_kernel(own_ref, other_ref, *refs):
    for d, out in enumerate(refs[-N_Z:]):
        out[...] = (own_ref[d].astype(f32) + other_ref[d].astype(f32)).astype(bf16)


def pair_sums(own, other, after):
    return pl.pallas_call(
        pair_kernel,
        out_shape=[pltpu.VMEM((PART, HALF), bf16)] + [pltpu.HBM((PART, HALF), bf16)] * (N_Z - 1),
        in_specs=[VMEM_SPEC, VMEM_SPEC] + [ANY_SPEC] * len(after),
        compiler_params=params(),
        name="pair_sums",
    )(own, other, *map(in_hbm, after))


def sum_kernel(*refs):
    total = refs[0][...].astype(f32)
    for term in refs[1:N_Z]:
        total += term[...].astype(f32)
    for out in refs[N_Z:]:
        out[...] = total.astype(bf16)


def sum_of(terms):
    return pl.pallas_call(
        sum_kernel,
        out_shape=both((PART, HALF)),
        compiler_params=params(),
        name="sum_over_z",
    )(*terms)


def advance_kernel(state_ref, own_ref, other_ref, gain_ref, *refs):
    next_send, next_ref, *messages = refs[-4:]
    update = own_ref[...].astype(f32) + other_ref[...].astype(f32)
    state = (state_ref[...].astype(f32) + update).astype(bf16)
    next_send[...] = state
    next_ref[...] = state
    message_of(state.astype(f32), gain_ref[...], messages)


def advance(state, own, other, gain, after):
    return pl.pallas_call(
        advance_kernel,
        out_shape=(*both((PART, HALF)), *both((MSG, HALF))),
        in_specs=[VMEM_SPEC] * 4 + [ANY_SPEC] * len(after),
        compiler_params=params(),
        name="advance",
    )(state, own, other, gain, *map(in_hbm, after))


def finish_kernel(place_ref, *refs):
    out_ref = refs[-1]
    for side in range(2):
        state, own, other = refs[3 * side : 3 * side + 3]
        update = own[...].astype(f32) + other[...].astype(f32)
        out_ref[half_of(place_ref[2] ^ side), :] = (state[...].astype(f32) + update).T.astype(bf16)


def finish(place, *sides):
    return pl.pallas_call(
        finish_kernel,
        out_shape=jax.ShapeDtypeStruct((TOK, PART), bf16),
        in_specs=[SMEM_SPEC] + [VMEM_SPEC] * 6,
        compiler_params=params(),
        name="finish",
    )(place, *sides)


def along_z(block, d):
    route = [(z * N_Q + q, (z + d) % N_Z * N_Q + q) for z in range(N_Z) for q in range(N_Q)]
    return lax.ppermute(block, "train", route)


def across_q(block, d):
    return lax.ppermute(block, "train", [(i, i ^ d) for i in range(N_TRAIN)])


def across_tp(block, d):
    return lax.ppermute(block, "tp", [(t, t ^ d) for t in range(4)])


def body(offsets, gate_flat, up_flat, down_flat, norm_gain, decode_state):
    width = norm_gain.shape[0]
    index = lax.axis_index("train")
    place = jnp.stack([index // N_Q, index % N_Q, lax.axis_index("tp") % 2]).astype(jnp.int32)
    q_groups = [[z * N_Q + q for q in range(N_Q)] for z in range(N_Z)]
    z_groups = [[z * N_Q + q for z in range(N_Z)] for q in range(N_Q)]

    heads = jnp.concatenate(
        [gate_flat[:, :GROUP], up_flat[:, :GROUP], down_flat[:, :GROUP], jnp.zeros((5, GROUP), f32)]
    )
    heads = lax.ppermute(heads, "train", [((i + 1) % N_TRAIN, i) for i in range(N_TRAIN)])
    gain = lax.dynamic_slice_in_dim(norm_gain, index * PART, PART, 0).reshape(PART, 1)
    state, first = begin(place, decode_state, gain)
    (first,) = release((first,), (heads,))
    first = lax.all_to_all(first, "train", 0, 0, tiled=True)

    gate, up, down = (flat.reshape(-1, GROUP) for flat in (gate_flat, up_flat, down_flat))
    low_strips, low_first = pack(0, offsets, gate, up, heads)
    high_strips, high_first = pack(Z_HALF, offsets, gate, up, heads)
    down_codes, down_scales, *down_served = code_down(offsets, place, down, heads, ())
    first, low_strips, *sent = release((first, low_strips, *down_served[1:]), (high_strips, high_first))
    other_first = across_tp(first, 1)
    low_strips = lax.all_to_all(low_strips, "train", 0, 0, axis_index_groups=q_groups, tiled=True)
    down_weights = [down_served[0]] + [along_z(sent[d - 1], d) for d in range(1, N_Z)]
    hidden, hidden_own = first_hidden(place, low_first, high_first, first, other_first, width)

    owned = []
    for step in range(STEPS):
        if step > 0:
            received = [along_z(message, d) for d in range(1, N_Z)]
            others = [across_tp(m, 1) for m in (message, *received)]
            *terms, held = gate_up_terms(
                place, low_served, high_served, (message_own, *received), others, turned[step - 1]
            )
            owned.append(lax.all_to_all(held, "train", 0, 0, axis_index_groups=z_groups, tiled=True))
            hidden, hidden_own = hidden_of([terms[0]] + [across_q(terms[d], d) for d in range(1, N_Q)], width)
        blocks = [hidden_own] + [across_q(hidden, d) for d in range(1, N_Q)]
        fetch = in_hbm if step == 1 else lambda array: array
        send, keep = update_terms(
            place, blocks, list(map(fetch, down_weights)), pltpu.HBM if step == 1 else pltpu.VMEM
        )
        after = ()
        if step == 0:
            (high_strips,) = release((high_strips,), (send,))
            high_strips = lax.all_to_all(high_strips, "train", 0, 0, axis_index_groups=q_groups, tiled=True)
            low_served, *turned = serve(0, place, low_strips, ())
            after = turned[:1]
            high_served, *turned = serve(1, place, high_strips, turned)
        sums = pair_sums(fetch(keep), fetch(across_tp(send, 1)), owned[-1:])
        total, total_own = sum_of([sums[0]] + [along_z(sums[d], -d) for d in range(1, N_Z)])
        other = across_tp(total, 2)
        if step < STEPS - 1:
            state_send, state, message, message_own = advance(state, total_own, other, gain, after)
        else:
            sides = (across_tp(state_send, 1), across_tp(total, 1), across_tp(total, 3))
            decoded = finish(place, state, total_own, other, *sides)
    gate_codes, gate_scales, up_codes, up_scales = split(*owned)
    return (gate_codes, gate_scales.T, up_codes, up_scales.T, down_codes, down_scales.T, decoded)


def solution(mesh):
    in_specs = (P(), P("tp", "train"), P("tp", "train"), P("tp", "train"), P(), P(None, "train"))
    out_specs = (
        P("tp", "train"),
        P("tp", "train"),
        P("tp", "train"),
        P("tp", "train"),
        P("train", "tp"),
        P("train", "tp"),
        P(None, "train"),
    )
    return jax.shard_map(body, mesh=mesh, in_specs=in_specs, out_specs=out_specs, check_vma=False)
```

```python
import functools

import jax
import jax.numpy as jnp
from jax import lax
from jax.experimental import pallas as pl
from jax.experimental.pallas import tpu as pltpu
from jax.sharding import PartitionSpec as P

GROUP = 128
STEPS = 3
EPSILON_SCALE = 1e-06
EPSILON_NORM = 1e-05

N_Z = 4
N_Q = 8
N_TRAIN = N_Z * N_Q
ROWS = 112
PART = 384
PER = PART // GROUP
GROUPS_ROW = N_TRAIN * PER
BLOCK = 16
STRIP = 2 * ROWS + BLOCK
FT = ROWS * N_TRAIN
DOWN_GROUPS = FT // GROUP
DOWN_PER = DOWN_GROUPS // N_Z
DOWN_BLOCK = 128
DOWN_BLOCKS = PART // DOWN_BLOCK
TOK = 256
MSG = PART + BLOCK
MIB = 1024 * 1024
HALF = TOK // 2
Z_HALF = N_Z // 2

bf16, f32 = jnp.bfloat16, jnp.float32


def params(mib=16):
    return pltpu.CompilerParams(vmem_limit_bytes=mib * MIB)


SMEM_SPEC = pl.BlockSpec(memory_space=pltpu.SMEM)
VMEM_SPEC = pl.BlockSpec(memory_space=pltpu.VMEM)
ANY_SPEC = pl.BlockSpec(memory_space=pl.ANY)


def in_hbm(array):
    return pltpu.with_memory_space_constraint(array, pltpu.HBM)


def in_vmem(array):
    return pltpu.with_memory_space_constraint(array, pltpu.VMEM)


def lanes_of(shape):
    return lax.broadcasted_iota(jnp.int32, shape, len(shape) - 1)


def following_rows(first, follow, turn):
    count = first.shape[0]
    up = pltpu.roll(first, count - 1, axis=0)
    row = lax.broadcasted_iota(jnp.int32, first.shape, 0)
    return pltpu.roll(jnp.where(row == count - 1, follow, up), turn, axis=1)


def scaled_group(group):
    scale = jnp.max(jnp.abs(group), axis=1, keepdims=True) + EPSILON_SCALE
    return scale, (group * (1.0 / scale)).astype(bf16)


def follow_of(step, last, next_ref, heads_ref, index):
    return jnp.where(step == last, heads_ref[index : index + 1, :], next_ref[0:1, :])


def pack_kernel(
    z_first, off_ref, gate_ref, gate_next, up_ref, up_next, heads_ref, out_ref, served_ref, kept_all, parts, rows
):
    step = pl.program_id(0)
    lane = lanes_of((ROWS, GROUP))
    last = (step == Z_HALF - 1) & (z_first > 0)
    kept_all[...] = jnp.zeros_like(kept_all)
    rows[...] = jnp.zeros_like(rows)
    for index, (x_ref, next_ref) in enumerate(((gate_ref, gate_next), (up_ref, up_next))):
        turn = GROUP - off_ref[index]
        own = lane < turn

        def turned(block):
            return pltpu.roll(block, turn, axis=1)

        after_row = next_ref[:, 0, :]
        wrapped = pltpu.roll(after_row, ROWS - 1, axis=0)
        row = lax.broadcasted_iota(jnp.int32, after_row.shape, 0)
        wrapped = jnp.where(row == ROWS - 1, heads_ref[index : index + 1, :], wrapped)
        follow = jnp.where(last, wrapped, after_row)
        kept = jnp.zeros((ROWS, GROUP), f32)
        current = turned(x_ref[:, 0, :])
        for g in range(N_Q * PER):
            after = turned(x_ref[:, g + 1, :] if g + 1 < N_Q * PER else follow)
            scale, codes = scaled_group(jnp.where(own, current, after))
            current = after
            q, k = g // PER, g % PER
            out_ref[q, 0, index * ROWS : (index + 1) * ROWS, k * GROUP : (k + 1) * GROUP] = codes
            served_ref[index * ROWS : (index + 1) * ROWS, g * GROUP : (g + 1) * GROUP] = (
                codes.astype(f32) * scale
            ).astype(bf16)
            kept = jnp.where(lane == q * 4 + k, scale, kept)
        kept_all[:ROWS, :] = kept
        rest = kept_all[...].T
        for part in range(3):
            piece = rest.astype(bf16).astype(f32)
            rest = rest - piece
            parts[...] = piece
            for k in range(PER):
                rows[k, pl.ds(index * 3 + part, N_Q, stride=BLOCK), :] = parts[pl.ds(k, N_Q, stride=4), :]
    for k in range(PER):
        out_ref[:, 0, 2 * ROWS :, k * GROUP : (k + 1) * GROUP] = (
            rows[k].reshape(N_Q, BLOCK, GROUP).astype(bf16)
        )


def pack(z_first, offsets, gate, up, heads):
    gate, up = (in_hbm(flat.reshape(ROWS, GROUPS_ROW, GROUP)) for flat in (gate, up))
    part = N_Q * PER
    main = pl.BlockSpec((ROWS, part, GROUP), lambda s, off: (0, s + z_first, 0))
    after = pl.BlockSpec((ROWS, 8, GROUP), lambda s, off: (0, lax.rem((s + z_first + 1) * (part // 8), GROUPS_ROW // 8), 0))
    return pl.pallas_call(
        functools.partial(pack_kernel, z_first),
        out_shape=(
            pltpu.HBM((N_Q, Z_HALF, STRIP, PART), bf16),
            pltpu.HBM((2 * ROWS, Z_HALF * part * GROUP), bf16),
        ),
        grid_spec=pltpu.PrefetchScalarGridSpec(
            num_scalar_prefetch=1,
            grid=(Z_HALF,),
            in_specs=[main, after, main, after, pl.BlockSpec((8, GROUP), lambda s, off: (0, 0))],
            out_specs=(
                pl.BlockSpec((N_Q, 1, STRIP, PART), lambda s, off: (0, s, 0, 0)),
                pl.BlockSpec((2 * ROWS, part * GROUP), lambda s, off: (0, s)),
            ),
            scratch_shapes=[
                pltpu.VMEM((GROUP, GROUP), f32),
                pltpu.VMEM((GROUP, GROUP), f32),
                pltpu.VMEM((PER, N_Q * BLOCK, GROUP), f32),
            ],
        ),
        compiler_params=params(24),
        name="pack_gate_up",
    )(offsets, gate, gate, up, up, heads)


def down_code_kernel(off_ref, place_ref, x_ref, next_ref, heads_ref, *refs):
    codes_ref, scales_ref, *served = refs[-2 - N_Z :]
    step = pl.program_id(0)
    turn = GROUP - off_ref[2]
    lane = lanes_of((DOWN_BLOCK, GROUP))
    own = lane < turn
    kept = jnp.zeros((DOWN_BLOCK, GROUP), f32)

    def column(g):
        return x_ref[pl.ds(g, DOWN_BLOCK, stride=DOWN_GROUPS), :]

    follow = follow_of(step, DOWN_BLOCKS - 1, next_ref, heads_ref, 2)
    wrapped = following_rows(column(0), follow, turn)
    for d, out in enumerate(served):
        z = lax.rem(place_ref[0] + d, N_Z)
        base = z * DOWN_PER
        current = pltpu.roll(column(base), turn, axis=1)
        for k in range(DOWN_PER):
            g = base + k
            if k + 1 < DOWN_PER:
                after = pltpu.roll(column(g + 1), turn, axis=1)
            else:
                after = pltpu.roll(column(jnp.minimum(g + 1, DOWN_GROUPS - 1)), turn, axis=1)
                after = jnp.where(z == N_Z - 1, wrapped, after)
            scale, codes = scaled_group(jnp.where(own, current, after))
            current = after
            codes_ref[:, pl.ds(pl.multiple_of(g * GROUP, GROUP), GROUP)] = codes
            out[:, k * GROUP : (k + 1) * GROUP] = (codes.astype(f32) * scale).astype(bf16)
            kept = jnp.where(lane == g, scale, kept)
    scales_ref[...] = kept.T[:DOWN_GROUPS, :]


def code_down(offsets, place, down, heads, after):
    block_groups = DOWN_BLOCK * DOWN_GROUPS
    last = PART * DOWN_GROUPS // 8 - 1
    return pl.pallas_call(
        down_code_kernel,
        out_shape=[
            jax.ShapeDtypeStruct((PART, FT), bf16),
            jax.ShapeDtypeStruct((DOWN_GROUPS, PART), f32),
        ]
        + [pltpu.HBM((PART, FT // N_Z), bf16)] * N_Z,
        grid_spec=pltpu.PrefetchScalarGridSpec(
            num_scalar_prefetch=2,
            grid=(DOWN_BLOCKS,),
            in_specs=[
                pl.BlockSpec((block_groups, GROUP), lambda s, *_: (s, 0)),
                pl.BlockSpec((8, GROUP), lambda s, *_: (jnp.minimum((s + 1) * (block_groups // 8), last), 0)),
                pl.BlockSpec((8, GROUP), lambda s, *_: (0, 0)),
            ]
            + [pl.BlockSpec(memory_space=pl.ANY)] * len(after),
            out_specs=[
                pl.BlockSpec((DOWN_BLOCK, FT), lambda s, *_: (s, 0)),
                pl.BlockSpec((DOWN_GROUPS, DOWN_BLOCK), lambda s, *_: (0, s)),
            ]
            + [pl.BlockSpec((DOWN_BLOCK, FT // N_Z), lambda s, *_: (s, 0))] * N_Z,
        ),
        compiler_params=params(),
        name="code_down",
    )(offsets, place, down, down, heads, *map(in_hbm, after))


def scale_columns(strip_of, count, gathered):
    gathered[...] = jnp.zeros_like(gathered)
    for n in range(count):
        tail = strip_of(n).astype(f32)
        for index in range(2):
            row = tail[3 * index : 3 * index + 1] + tail[3 * index + 1 : 3 * index + 2]
            row = row + tail[3 * index + 2 : 3 * index + 3]
            for k in range(PER):
                at = (n * 2 + index) * PER + k
                gathered[at : at + 1, :] = row[:, k * GROUP : (k + 1) * GROUP]
    return gathered[...].T


def serve_kernel(place_ref, in_ref, *refs):
    served_ref, gate_ref, up_ref, gathered = refs[-4:]
    columns = scale_columns(lambda n: in_ref[0, n, 2 * ROWS : STRIP, :], Z_HALF, gathered)
    for z in range(Z_HALF):
        gate_ref[z, 0] = in_ref[0, z, :ROWS]
        up_ref[z, 0] = in_ref[0, z, ROWS:]
        for index in range(2):
            for k in range(PER):
                at = (z * 2 + index) * PER + k
                codes = in_ref[0, z, index * ROWS : (index + 1) * ROWS, k * GROUP : (k + 1) * GROUP]
                start = pl.multiple_of(pl.program_id(0) * 2 * ROWS + index * ROWS, BLOCK)
                served_ref[pl.ds(start, ROWS), z * PART + k * GROUP : z * PART + (k + 1) * GROUP] = (
                    codes.astype(f32) * columns[:ROWS, at : at + 1]
                ).astype(bf16)


def serve(half, place, strips, turned):
    return pl.pallas_call(
        serve_kernel,
        out_shape=(
            pltpu.VMEM((N_Q * 2 * ROWS, Z_HALF * PART), bf16),
            pltpu.HBM((N_Z, N_Q, ROWS, PART), bf16),
            pltpu.HBM((N_Z, N_Q, STRIP - ROWS, PART), bf16),
        ),
        grid_spec=pltpu.PrefetchScalarGridSpec(
            num_scalar_prefetch=1,
            grid=(N_Q,),
            in_specs=[pl.BlockSpec((1, Z_HALF, STRIP, PART), lambda s, place: (s ^ place[1], 0, 0, 0))]
            + [pl.BlockSpec(memory_space=pl.ANY)] * len(turned),
            out_specs=(
                VMEM_SPEC,
                pl.BlockSpec((Z_HALF, 1, ROWS, PART), lambda s, place: (half, s ^ place[1], 0, 0)),
                pl.BlockSpec((Z_HALF, 1, STRIP - ROWS, PART), lambda s, place: (half, s ^ place[1], 0, 0)),
            ),
            scratch_shapes=[pltpu.VMEM((GROUP, GROUP), f32)],
        ),
        input_output_aliases={2 + n: 1 + n for n in range(len(turned))},
        compiler_params=params(),
        name="serve_gate_up",
    )(place, in_hbm(strips), *turned)


SPLIT = 8


def scale_row(tail, index):
    parts = tail[3 * index : 3 * index + 3].astype(f32)
    return parts[0:1] + parts[1:2] + parts[2:3]


def split_kernel(gate_in, up_in, gate_ref, gate_scales, up_ref, up_scales, rows):
    lane = lanes_of((8, GROUP))
    blocks = SPLIT * ROWS // GROUP
    for index, scales in enumerate((gate_scales, up_scales)):
        sums = [jnp.zeros((8, GROUP), f32) for _ in range(blocks)]
        for n in range(SPLIT):
            row = scale_row(up_in[n, ROWS:, :], index)
            rows[...] = jnp.zeros_like(rows)
            for k in range(PER):
                rows[k : k + 1, :] = row[:, k * GROUP : (k + 1) * GROUP]
            block, offset = n * ROWS // GROUP, n * ROWS % GROUP
            moved = jnp.where(lane < ROWS, rows[...], 0.0)
            moved = pltpu.roll(moved, offset, axis=1) if offset else moved
            sums[block] = sums[block] + jnp.where(lane >= offset, moved, 0.0)
            if offset + ROWS > GROUP:
                sums[block + 1] = sums[block + 1] + jnp.where(lane < offset, moved, 0.0)
        for block in range(blocks):
            scales[:, block * GROUP : (block + 1) * GROUP] = sums[block][:PER, :]
    for n in range(SPLIT):
        gate_ref[n * ROWS : (n + 1) * ROWS, :] = gate_in[n]
        up_ref[n * ROWS : (n + 1) * ROWS, :] = up_in[n, :ROWS]


def split(gate, up):
    codes = pltpu.HBM((FT, PART), bf16)
    scales = pltpu.HBM((PER, FT), f32)
    rows = SPLIT * ROWS
    return pl.pallas_call(
        split_kernel,
        out_shape=(codes, scales, codes, scales),
        grid=(N_TRAIN // SPLIT,),
        in_specs=[
            pl.BlockSpec((SPLIT, ROWS, PART), lambda s: (s, 0, 0)),
            pl.BlockSpec((SPLIT, STRIP - ROWS, PART), lambda s: (s, 0, 0)),
        ],
        out_specs=(
            pl.BlockSpec((rows, PART), lambda s: (s, 0)),
            pl.BlockSpec((PER, rows), lambda s: (0, s)),
            pl.BlockSpec((rows, PART), lambda s: (s, 0)),
            pl.BlockSpec((PER, rows), lambda s: (0, s)),
        ),
        scratch_shapes=[pltpu.VMEM((8, GROUP), f32)],
        compiler_params=params(),
        name="split_gate_up",
    )(in_hbm(gate.reshape(N_TRAIN, ROWS, PART)), in_hbm(up.reshape(N_TRAIN, STRIP - ROWS, PART)))


def two_parts(row):
    high = row.astype(bf16).astype(f32)
    at = lax.broadcasted_iota(jnp.int32, (BLOCK, row.shape[1]), 0)
    return jnp.where(at == 0, high, jnp.where(at == 1, row - high, 0.0)).astype(bf16)


def message_of(state, gain, refs):
    scaled, squares = (state * gain).astype(bf16), two_parts(jnp.sum(state * state, axis=0, keepdims=True))
    for ref in refs:
        ref[:PART, :] = scaled
        ref[PART:, :] = squares


def both(shape):
    return pltpu.HBM(shape, bf16), pltpu.VMEM(shape, bf16)


def half_of(core):
    return pl.ds(pl.multiple_of(core * HALF, HALF), HALF)


def begin_kernel(place_ref, state_ref, gain_ref, state_out, out_ref):
    half = state_ref[half_of(place_ref[2]), :].astype(f32).T
    state_out[...] = half.astype(bf16)
    message_of(half, gain_ref[...], [out_ref.at[n] for n in range(N_TRAIN)])


def begin(place, state, gain):
    return pl.pallas_call(
        begin_kernel,
        out_shape=(pltpu.HBM((PART, HALF), bf16), pltpu.HBM((N_TRAIN, MSG, HALF), bf16)),
        in_specs=[SMEM_SPEC, VMEM_SPEC, VMEM_SPEC],
        compiler_params=params(),
        name="begin",
    )(place, state, gain)


def release_kernel(*refs):
    del refs


def release(arrays, after):
    return pl.pallas_call(
        release_kernel,
        out_shape=[pltpu.HBM(a.shape, a.dtype) for a in arrays],
        in_specs=[ANY_SPEC] * (len(arrays) + len(after)),
        out_specs=[ANY_SPEC] * len(arrays),
        input_output_aliases={n: n for n in range(len(arrays))},
        compiler_params=params(),
        name="release",
    )(*arrays, *map(in_hbm, after))


def activated(total, squares, width):
    inverse = lax.rsqrt(squares / width + EPSILON_NORM)
    gate = total[:ROWS] * inverse
    up = total[ROWS : 2 * ROWS] * inverse
    return (gate / (1.0 + jnp.exp(-gate)) * up).astype(bf16)


FIRST = 4


def first_kernel(width, place_ref, low_ref, high_ref, own_ref, other_ref, *refs):
    outs, (total, squares) = refs[:2], refs[2:]
    step = pl.program_id(0)
    in_low = step < N_TRAIN // FIRST // 2

    @pl.when(step == 0)
    def _():
        total[...] = jnp.zeros_like(total)
        squares[...] = jnp.zeros_like(squares)

    for side, x_ref in enumerate((own_ref, other_ref)):
        lanes = slice(side * HALF, (side + 1) * HALF)
        inputs = jnp.concatenate([x_ref[n, :PART, :] for n in range(FIRST)], axis=0)
        for near, weight_ref in ((in_low, low_ref), (~in_low, high_ref)):

            @pl.when(near)
            def _():
                total[:, lanes] += jnp.dot(weight_ref[...], inputs, preferred_element_type=f32)

        for n in range(FIRST):
            tail = x_ref[n, PART:, :].astype(f32)
            squares[0:1, lanes] += tail[0:1] + tail[1:2]

    @pl.when(step == N_TRAIN // FIRST - 1)
    def _():
        hidden = activated(total[...], squares[0:1, :], width)
        core = place_ref[2]
        for side in range(2):
            at = pl.multiple_of((core ^ side) * HALF, HALF)
            for out in outs:
                out[:, pl.ds(at, HALF)] = hidden[:, side * HALF : (side + 1) * HALF]


def first_hidden(place, low, high, own, other, width):
    inputs = pl.BlockSpec((FIRST, MSG, HALF), lambda s, place: (s, 0, 0))
    steps = N_TRAIN // FIRST
    return pl.pallas_call(
        functools.partial(first_kernel, float(width)),
        out_shape=both((ROWS, TOK)),
        grid_spec=pltpu.PrefetchScalarGridSpec(
            num_scalar_prefetch=1,
            grid=(steps,),
            in_specs=[
                pl.BlockSpec((2 * ROWS, FIRST * PART), lambda s, place: (0, jnp.minimum(s, steps // 2 - 1))),
                pl.BlockSpec((2 * ROWS, FIRST * PART), lambda s, place: (0, jnp.maximum(s - steps // 2, 0))),
                inputs,
                inputs,
            ],
            out_specs=[pl.BlockSpec((ROWS, TOK), lambda s, place: (0, 0))] * 2,
            scratch_shapes=[pltpu.VMEM((2 * ROWS, TOK), f32), pltpu.VMEM((8, TOK), f32)],
        ),
        compiler_params=params(),
        name="first_hidden",
    )(place, *map(in_hbm, (low, high, own, other)))


def terms_kernel(place_ref, low_ref, high_ref, *refs):
    own, other, outs, inputs = refs[:N_Z], refs[N_Z : 2 * N_Z], refs[-N_Q - 2 : -2], refs[-1]
    core = place_ref[2]
    squares = []
    for side, messages in enumerate((own, other)):
        lanes = half_of(core ^ side)
        total = jnp.zeros((1, HALF), f32)
        for d, message in enumerate(messages):
            at = pl.multiple_of(lax.rem(place_ref[0] - d + N_Z, N_Z) * PART, PART)
            inputs[pl.ds(at, PART), lanes] = message[:PART, :]
            tail = message[PART:, :].astype(f32)
            total += tail[0:1] + tail[1:2]
        squares.append(total)
    middle = Z_HALF * PART
    for d, out in enumerate(outs):
        rows = slice(d * 2 * ROWS, (d + 1) * 2 * ROWS)
        total = jnp.dot(low_ref[rows, :], inputs[:middle, :], preferred_element_type=f32)
        total += jnp.dot(high_ref[rows, :], inputs[middle:, :], preferred_element_type=f32)
        out[: 2 * ROWS, :] = total.astype(bf16)
        for side in range(2):
            out[2 * ROWS :, half_of(core ^ side)] = two_parts(squares[side])


def gate_up_terms(place, low, high, own, other, held):
    return pl.pallas_call(
        terms_kernel,
        out_shape=[pltpu.VMEM((STRIP, TOK), bf16)]
        + [pltpu.HBM((STRIP, TOK), bf16)] * (N_Q - 1)
        + [pltpu.HBM(held.shape, held.dtype)],
        in_specs=[SMEM_SPEC] + [VMEM_SPEC] * (2 + 2 * N_Z) + [ANY_SPEC],
        out_specs=[VMEM_SPEC] * N_Q + [ANY_SPEC],
        scratch_shapes=[pltpu.VMEM((N_Z * PART, TOK), bf16)],
        input_output_aliases={3 + 2 * N_Z: N_Q},
        compiler_params=params(),
        name="gate_up_terms",
    )(place, in_vmem(low), in_vmem(high), *own, *other, held)


def hidden_kernel(width, *refs):
    total = refs[0][...].astype(f32)
    for term in refs[1:N_Q]:
        total += term[...].astype(f32)
    squares = total[2 * ROWS : 2 * ROWS + 1] + total[2 * ROWS + 1 : 2 * ROWS + 2]
    hidden = activated(total, squares, width)
    for out in refs[N_Q:]:
        out[...] = hidden


def hidden_of(terms, width):
    return pl.pallas_call(
        functools.partial(hidden_kernel, float(width)),
        out_shape=both((ROWS, TOK)),
        compiler_params=params(),
        name="hidden",
    )(*terms)


def update_kernel(place_ref, *refs):
    hidden, weights = refs[:N_Q], refs[N_Q : N_Q + N_Z]
    send_ref, keep_ref, joined, result = refs[-4:]
    for d, block in enumerate(hidden):
        at = pl.multiple_of((place_ref[1] ^ d) * ROWS, BLOCK)
        joined[pl.ds(at, ROWS), :] = block[...]
    core = place_ref[2]
    for d, weight in enumerate(weights):
        result[d] = jnp.dot(weight[...], joined[...], preferred_element_type=f32).astype(bf16)
        send_ref[d] = result[d, :, half_of(core ^ 1)]
        keep_ref[d] = result[d, :, half_of(core)]


def update_terms(place, hidden, weights, kept):
    return pl.pallas_call(
        update_kernel,
        out_shape=(pltpu.HBM((N_Z, PART, HALF), bf16), kept((N_Z, PART, HALF), bf16)),
        in_specs=[SMEM_SPEC] + [VMEM_SPEC] * (N_Q + N_Z),
        scratch_shapes=[pltpu.VMEM((FT // N_Z, TOK), bf16), pltpu.VMEM((N_Z, PART, TOK), bf16)],
        compiler_params=params(),
        name="update_terms",
    )(place, *hidden, *weights)


def pair_kernel(own_ref, other_ref, *refs):
    for d, out in enumerate(refs[-N_Z:]):
        out[...] = (own_ref[d].astype(f32) + other_ref[d].astype(f32)).astype(bf16)


def pair_sums(own, other, after):
    return pl.pallas_call(
        pair_kernel,
        out_shape=[pltpu.VMEM((PART, HALF), bf16)] + [pltpu.HBM((PART, HALF), bf16)] * (N_Z - 1),
        in_specs=[VMEM_SPEC, VMEM_SPEC] + [ANY_SPEC] * len(after),
        compiler_params=params(),
        name="pair_sums",
    )(own, other, *map(in_hbm, after))


def sum_kernel(*refs):
    total = refs[0][...].astype(f32)
    for term in refs[1:N_Z]:
        total += term[...].astype(f32)
    for out in refs[N_Z:]:
        out[...] = total.astype(bf16)


def sum_of(terms):
    return pl.pallas_call(
        sum_kernel,
        out_shape=both((PART, HALF)),
        compiler_params=params(),
        name="sum_over_z",
    )(*terms)


def advance_kernel(state_ref, own_ref, other_ref, gain_ref, *refs):
    next_send, next_ref, *messages = refs[-4:]
    update = own_ref[...].astype(f32) + other_ref[...].astype(f32)
    state = (state_ref[...].astype(f32) + update).astype(bf16)
    next_send[...] = state
    next_ref[...] = state
    message_of(state.astype(f32), gain_ref[...], messages)


def advance(state, own, other, gain, after):
    return pl.pallas_call(
        advance_kernel,
        out_shape=(*both((PART, HALF)), *both((MSG, HALF))),
        in_specs=[VMEM_SPEC] * 4 + [ANY_SPEC] * len(after),
        compiler_params=params(),
        name="advance",
    )(state, own, other, gain, *map(in_hbm, after))


def finish_kernel(place_ref, *refs):
    out_ref = refs[-1]
    for side in range(2):
        state, own, other = refs[3 * side : 3 * side + 3]
        update = own[...].astype(f32) + other[...].astype(f32)
        out_ref[half_of(place_ref[2] ^ side), :] = (state[...].astype(f32) + update).T.astype(bf16)


def finish(place, *sides):
    return pl.pallas_call(
        finish_kernel,
        out_shape=jax.ShapeDtypeStruct((TOK, PART), bf16),
        in_specs=[SMEM_SPEC] + [VMEM_SPEC] * 6,
        compiler_params=params(),
        name="finish",
    )(place, *sides)


def along_z(block, d):
    route = [(z * N_Q + q, (z + d) % N_Z * N_Q + q) for z in range(N_Z) for q in range(N_Q)]
    return lax.ppermute(block, "train", route)


def across_q(block, d):
    return lax.ppermute(block, "train", [(i, i ^ d) for i in range(N_TRAIN)])


def across_tp(block, d):
    return lax.ppermute(block, "tp", [(t, t ^ d) for t in range(4)])


def body(offsets, gate_flat, up_flat, down_flat, norm_gain, decode_state):
    width = norm_gain.shape[0]
    index = lax.axis_index("train")
    place = jnp.stack([index // N_Q, index % N_Q, lax.axis_index("tp") % 2]).astype(jnp.int32)
    q_groups = [[z * N_Q + q for q in range(N_Q)] for z in range(N_Z)]
    z_groups = [[z * N_Q + q for z in range(N_Z)] for q in range(N_Q)]

    heads = jnp.concatenate(
        [gate_flat[:, :GROUP], up_flat[:, :GROUP], down_flat[:, :GROUP], jnp.zeros((5, GROUP), f32)]
    )
    heads = lax.ppermute(heads, "train", [((i + 1) % N_TRAIN, i) for i in range(N_TRAIN)])
    gain = lax.dynamic_slice_in_dim(norm_gain, index * PART, PART, 0).reshape(PART, 1)
    state, first = begin(place, decode_state, gain)
    (first,) = release((first,), (heads,))
    first = lax.all_to_all(first, "train", 0, 0, tiled=True)

    gate, up, down = (flat.reshape(-1, GROUP) for flat in (gate_flat, up_flat, down_flat))
    low_strips, low_first = pack(0, offsets, gate, up, heads)
    high_strips, high_first = pack(Z_HALF, offsets, gate, up, heads)
    down_codes, down_scales, *down_served = code_down(offsets, place, down, heads, ())
    first, low_strips, *sent = release((first, low_strips, *down_served[1:]), (high_strips, high_first))
    other_first = across_tp(first, 1)
    low_strips = lax.all_to_all(low_strips, "train", 0, 0, axis_index_groups=q_groups, tiled=True)
    down_weights = [down_served[0]] + [along_z(sent[d - 1], d) for d in range(1, N_Z)]
    hidden, hidden_own = first_hidden(place, low_first, high_first, first, other_first, width)

    owned = []
    for step in range(STEPS):
        if step > 0:
            received = [along_z(message, d) for d in range(1, N_Z)]
            others = [across_tp(m, 1) for m in (message, *received)]
            *terms, held = gate_up_terms(
                place, low_served, high_served, (message_own, *received), others, turned[step - 1]
            )
            owned.append(lax.all_to_all(held, "train", 0, 0, axis_index_groups=z_groups, tiled=True))
            hidden, hidden_own = hidden_of([terms[0]] + [across_q(terms[d], d) for d in range(1, N_Q)], width)
        blocks = [hidden_own] + [across_q(hidden, d) for d in range(1, N_Q)]
        fetch = in_hbm if step == 1 else lambda array: array
        send, keep = update_terms(
            place, blocks, list(map(fetch, down_weights)), pltpu.HBM if step == 1 else pltpu.VMEM
        )
        after = ()
        if step == 0:
            (high_strips,) = release((high_strips,), (send,))
            high_strips = lax.all_to_all(high_strips, "train", 0, 0, axis_index_groups=q_groups, tiled=True)
            low_served, *turned = serve(0, place, low_strips, ())
            after = turned[:1]
            high_served, *turned = serve(1, place, high_strips, turned)
        sums = pair_sums(fetch(keep), fetch(across_tp(send, 1)), owned[-1:])
        total, total_own = sum_of([sums[0]] + [along_z(sums[d], -d) for d in range(1, N_Z)])
        other = across_tp(total, 2)
        if step < STEPS - 1:
            state_send, state, message, message_own = advance(state, total_own, other, gain, after)
        else:
            sides = (across_tp(state_send, 1), across_tp(total, 1), across_tp(total, 3))
            decoded = finish(place, state, total_own, other, *sides)
    gate_codes, gate_scales, up_codes, up_scales = split(*owned)
    return (gate_codes, gate_scales.T, up_codes, up_scales.T, down_codes, down_scales.T, decoded)


def solution(mesh):
    in_specs = (P(), P("tp", "train"), P("tp", "train"), P("tp", "train"), P(), P(None, "train"))
    out_specs = (
        P("tp", "train"),
        P("tp", "train"),
        P("tp", "train"),
        P("tp", "train"),
        P("train", "tp"),
        P("train", "tp"),
        P(None, "train"),
    )
    return jax.shard_map(body, mesh=mesh, in_specs=in_specs, out_specs=out_specs, check_vma=False)
```
